32 devices in a mesh: dp: 8 (over z, x), rep: 4 (over y, core).
Axes of the slice: x: 2, y: 2, z: 4, core: 2. Of those that a mesh axis runs over, the one named last changes fastest.
Arguments:
- events: bfloat16 [16384, 512], P(('dp', 'rep')), may hold values from -6 to 6
- grad_out: bfloat16 [16384, 512], P(('dp', 'rep')), may hold values from -15 to 15
- w_uvqk: bfloat16 [512, 2048], replicated, may hold values from -0.25 to 0.25
- w_out: bfloat16 [512, 512], replicated, may hold values from -0.25 to 0.25
- send_place: int32 [32, 512], P(('dp', 'rep')), may hold values from 0 to 1023, as said below
- send_counts: int32 [32, 8], P(('dp', 'rep')), may hold values from 0 to 128, as said below
- user_ids: int32 [32, 512], P(('dp', 'rep')), may hold values from 0 to 15, never falling along the last dimension, each value on 1 to 256 neighbouring positions
Outputs:
- grad_events: bfloat16 [16384, 512], P(('dp', 'rep'))
- grad_w_uvqk: float32 [512, 2048], P(None, 'dp')
- grad_w_out: float32 [512, 512], P(None, 'dp')
The draws below stay inside these ranges and needn't reach their ends.
Inputs may be any that keep to these rules, and one draw needn't show every extreme that they name: `send_counts`: row d * 4 + r gives, for each owner o of group r, how many events device (d, r) sends there; each row sums to 512, and the counts one owner receives from the 8 devices of its group also sum to 512. `send_place`: an event bound for owner o has place o * 128 + j, where j runs from 0 to that owner's count minus 1 over the device's events bound for o; each place at most once on a device. `user_ids`: each row lists an owner's users in the owner's order of events; ids never fall.
All inputs are finite; a program needn't handle non-finite values.
Results may differ from the reference program's by a relative error of at most 0.02.
Values may be sent and summed in bfloat16 or wider, within the bound.
No kernel may reach another device: no remote copies, remote signals or barrier semaphores. Data moves between devices by JAX's collectives and lax.ppermute only.
A program may use at most 192 MiB of HBM per device.

```python
import math
import jax
import jax.numpy as jnp
import numpy as np
from jax import lax

D = 512
HEADS = 8
EV_DEV = 512
CAP = 128
USERS = 16
LEN_MOST = 256
EVENTS = 16384
N_DP = 8
N_REP = 4


def routing_tables(key):
    owners = N_DP
    groups = N_REP
    mean_count = EV_DEV // N_DP
    deltas = jax.random.randint(jax.random.fold_in(key, 11), (groups, owners // 2), 0, mean_count // 2 + 1)
    deltas = deltas.at[:, 0].set(mean_count)
    profile = jnp.stack([mean_count + deltas, mean_count - deltas], axis=-1).reshape(groups, owners)
    shifts = jax.random.randint(jax.random.fold_in(key, 12), (groups,), 0, owners)
    rolled = (jnp.arange(owners)[None, :] - shifts[:, None]) % owners
    profile = jnp.take_along_axis(profile, rolled, axis=1)
    blocks = jnp.arange(owners * groups)
    source = blocks // groups
    group = blocks % groups
    column = (jnp.arange(owners)[None, :] - source[:, None]) % owners
    counts = profile[group[:, None], column].astype(jnp.int32)
    ends = jnp.cumsum(counts, axis=1).astype(jnp.int32)
    starts = ends - counts
    target_positions = jnp.arange(EV_DEV, dtype=jnp.int32)
    owner_of = jnp.sum((target_positions[None, :, None] >= ends[:, None, :]).astype(jnp.int32), axis=2)
    first = jnp.take_along_axis(starts, owner_of, axis=1)
    slots = owner_of * CAP + target_positions[None, :] - first
    keys = jax.random.split(jax.random.fold_in(key, 13), owners * groups)
    sorting_orders = jax.vmap(lambda single: jax.random.permutation(single, EV_DEV))(keys)
    slots = jnp.take_along_axis(slots, sorting_orders, axis=1)
    return (counts, slots.astype(jnp.int32))


def draw_send_counts(key, part):
    return routing_tables(key)[0]


def draw_send_place(key, part):
    return routing_tables(key)[1]


def zero_rows(key):
    counts, slots = routing_tables(key)
    blocks = N_DP * N_REP
    owner_of = slots // CAP
    within = slots - owner_of * CAP
    last_of = jnp.take_along_axis(counts, owner_of, axis=1) - 1
    picked = jax.random.randint(jax.random.fold_in(key, 14), (blocks, N_DP), 0, 4) == 0
    device_rows = jnp.arange(blocks, dtype=jnp.int32)
    picked = picked | (jnp.arange(N_DP, dtype=jnp.int32)[None, :] == (device_rows % N_DP)[:, None])
    chosen = jnp.take_along_axis(picked, owner_of, axis=1) & (within == last_of)
    keep = jnp.where(chosen, 0.0, 1.0).astype(jnp.float32)
    return keep.reshape(EVENTS, 1)


def draw_events(key, part):
    value_key = jax.random.fold_in(key, 21)
    values = jax.random.truncated_normal(value_key, -6.0, 6.0, (EVENTS, D), jnp.float32)
    return (values * zero_rows(key)).astype(jnp.bfloat16)


def draw_grad_out(key, part):
    value_key = jax.random.fold_in(key, 22)
    blocks = N_DP * N_REP
    values = jax.random.truncated_normal(value_key, -6.0, 6.0, (EVENTS, D), jnp.float32)
    pairing = jax.random.permutation(jax.random.fold_in(key, 23), N_DP)
    device_rows = jnp.arange(blocks, dtype=jnp.int32)
    target_block = pairing[(device_rows // N_REP + device_rows % N_REP) % N_DP]
    column_block = jnp.arange(D, dtype=jnp.int32) // (D // N_DP)
    boost = jnp.where(column_block[None, :] == target_block[:, None], 2.5, 1.0).astype(jnp.float32)
    values = (values.reshape(blocks, EV_DEV, D) * boost[:, None, :]).reshape(EVENTS, D)
    return (values * zero_rows(key)).astype(jnp.bfloat16)


def length_profile(count, total, most, slope):
    loads = [(1 << 20) // math.isqrt(grade ** slope) + 1 for grade in range(2, count + 1)]
    surplus, given = total - most - (count - 1), [1] * (count - 1)
    while surplus > 0:
        candidates = [i for i in range(count - 1) if given[i] < most]
        pool, budget = sum([loads[i] for i in candidates]), surplus
        for i in candidates:
            addition = min(most - given[i], max(1, budget * loads[i] // pool), surplus)
            given[i] = given[i] + addition
            surplus = surplus - addition
    return np.array([most] + given)


def ragged_sizes(stream_key, amount, total, most, slope):
    if amount == 2:
        one = jax.random.randint(stream_key, (), max(1, total - most), min(most, total - 1) + 1)
        return jnp.stack([one, total - one])
    sizes = jnp.asarray(length_profile(amount, total, most, slope), jnp.int32)
    couples = (amount - 1) // 2
    giver, taker = sizes[1:1 + 2 * couples:2], sizes[2:2 + 2 * couples:2]
    slack = jnp.minimum(giver - 1, most - taker)
    passed = jax.random.randint(jax.random.fold_in(stream_key, 1), (couples,), 0, 1 << 20) % (slack + 1)
    sizes = sizes.at[1:1 + 2 * couples:2].set(giver - passed).at[2:2 + 2 * couples:2].set(taker + passed)
    return sizes[jax.random.permutation(jax.random.fold_in(stream_key, 2), amount)]


def centred(own_key, dims, scale, most, kind=jnp.bfloat16):
    values = jax.random.normal(own_key, dims, jnp.float32) * scale
    return jnp.minimum(jnp.maximum(values, -most), most).astype(kind)


def setup_inputs(seed: int = 0) -> dict:
    seeds = jax.random.split(jax.random.key(seed), 8)
    return {
        "events": draw_events(jax.random.fold_in(seeds[7], 71), 0),
        "grad_out": draw_grad_out(jax.random.fold_in(seeds[7], 71), 0),
        "w_uvqk": centred(seeds[2], (D, 4 * D), D ** -0.5, 0.25),
        "w_out": centred(seeds[3], (D, D), D ** -0.5, 0.25),
        "send_place": draw_send_place(jax.random.fold_in(seeds[7], 71), 0),
        "send_counts": draw_send_counts(jax.random.fold_in(seeds[7], 71), 0),
        "user_ids": jax.vmap(lambda own: jnp.searchsorted(jnp.cumsum(ragged_sizes(own, USERS, EV_DEV, LEN_MOST, 2)), jnp.arange(EV_DEV), side="right"))(jax.random.split(seeds[6], (N_DP * N_REP))).reshape((N_DP * N_REP, EV_DEV)).astype(jnp.int32),
    }


EPSILON = 1e-05

def normalized_row_block(values):
    center = values - lax.optimization_barrier(jnp.mean(values, axis=-1, keepdims=True))
    spread = lax.optimization_barrier(jnp.mean(center * center, axis=-1, keepdims=True))
    return center * lax.rsqrt(spread + EPSILON)

def hstu_layer(event_row_block, input_weight_matrix, weight_out, allowed):
    width = weight_out.shape[0]
    count = event_row_block.shape[0]
    head_size = width // HEADS
    normalized_input = normalized_row_block(event_row_block.astype(jnp.float32)).astype(jnp.bfloat16)
    activation_value = jax.nn.silu(jnp.dot(normalized_input, input_weight_matrix, preferred_element_type=jnp.float32)).astype(jnp.bfloat16)
    gate_u = activation_value[:, :width]
    values = activation_value[:, width:2 * width].reshape(count, HEADS, head_size)
    queries = activation_value[:, 2 * width:3 * width].reshape(count, HEADS, head_size)
    keys = activation_value[:, 3 * width:].reshape(count, HEADS, head_size)
    scores = jnp.einsum('qhd,khd->hqk', queries.astype(jnp.float32), keys.astype(jnp.float32)) * head_size ** (-0.5)
    weights = (jax.nn.silu(scores) * allowed[None]).astype(jnp.bfloat16)
    attended = jnp.einsum('hqk,khd->qhd', weights.astype(jnp.float32), values.astype(jnp.float32)).reshape(count, width)
    gated = (normalized_row_block(attended) * gate_u.astype(jnp.float32)).astype(jnp.bfloat16)
    return event_row_block.astype(jnp.float32) + jnp.dot(gated, weight_out, preferred_element_type=jnp.float32)

def owner_grads(event_row_block, cotangent, input_weight_matrix, weight_out, allowed):
    result, pullback = jax.vjp(lambda first, second, third: hstu_layer(first, second, third, allowed), event_row_block, input_weight_matrix, weight_out)
    return pullback(cotangent.astype(jnp.float32))

def compact_index(counts_in, owned, capacity):
    ends = jnp.cumsum(counts_in).astype(jnp.int32)
    starts = (ends - counts_in).astype(jnp.int32)
    target_positions = jnp.arange(owned, dtype=jnp.int32)
    source = lax.optimization_barrier(jnp.sum((target_positions[:, None] >= ends[None, :]).astype(jnp.int32), axis=1)).astype(jnp.int32)
    onehot = (jnp.arange(counts_in.shape[0], dtype=jnp.int32)[None, :] == source[:, None]).astype(jnp.int32)
    first = lax.optimization_barrier(jnp.sum(onehot * starts[None, :], axis=1)).astype(jnp.int32)
    return (source * capacity + target_positions - first).astype(jnp.int32)

def reference(events, grad_out, w_uvqk, w_out, send_place, send_counts, user_ids):
    owners = N_DP
    groups = N_REP
    width = D

    def spread_rows(event_row_block):
        blocks = event_row_block.reshape(owners * groups, EV_DEV, width)
        buffers = jax.vmap(lambda part, place: jnp.zeros((owners * CAP, width), part.dtype).at[place].set(part))(blocks, send_place)
        buffers = buffers.reshape(owners, groups, owners, CAP, width)
        return buffers.transpose(2, 1, 0, 3, 4).reshape(owners * groups, owners * CAP, width)
    recv_x = spread_rows(events)
    recv_dy = spread_rows(grad_out)
    count_cols = send_counts.reshape(owners, groups, owners).transpose(2, 1, 0).reshape(owners * groups, owners)

    def step(carry, inputs):
        rows_x, rows_dy, counts_in, users = inputs
        order_index = compact_index(counts_in, EV_DEV, CAP)
        owned_x = jnp.take(rows_x, order_index, axis=0)
        owned_dy = jnp.take(rows_dy, order_index, axis=0)
        target_positions = jnp.arange(EV_DEV, dtype=jnp.int32)
        allowed = ((users[:, None] == users[None, :]) & (target_positions[None, :] <= target_positions[:, None])).astype(jnp.float32)
        grad_x, grad_in, grad_outw = owner_grads(owned_x, owned_dy, w_uvqk, w_out, allowed)
        padded = jnp.zeros((owners * CAP, width), jnp.bfloat16).at[order_index].set(grad_x)
        return ((carry[0] + grad_in.astype(jnp.float32), carry[1] + grad_outw.astype(jnp.float32)), padded)
    start = (jnp.zeros((width, 4 * width), jnp.float32), jnp.zeros((width, width), jnp.float32))
    sums, padded_all = lax.scan(step, start, (recv_x, recv_dy, count_cols, user_ids))
    back = padded_all.reshape(owners, groups, owners, CAP, width).transpose(2, 1, 0, 3, 4)
    back = back.reshape(owners * groups, owners * CAP, width)
    grad_events = jax.vmap(lambda buffer, place: jnp.take(buffer, place, axis=0))(back, send_place)
    return (grad_events.reshape(owners * groups * EV_DEV, width), sums[0], sums[1])
```

```python
import functools

import jax
import jax.numpy as jnp
from jax import lax
from jax.experimental import pallas as pl
from jax.experimental.pallas import tpu as pltpu
from jax.sharding import PartitionSpec as P

HEADS = 8
LONGEST = 256
EPSILON = 1e-05
EMPTY = 128.0
BLOCK = 128
LANES = 128
F32 = jnp.float32
BF16 = jnp.bfloat16
VMEM_LIMIT = 40 * 1024 * 1024


def dot(a, b):
    return jnp.dot(a, b, preferred_element_type=F32)


def dot_nt(a, b):
    return lax.dot_general(a, b, (((1,), (1,)), ((), ())), preferred_element_type=F32)


def iota(shape, dim):
    return lax.broadcasted_iota(jnp.int32, shape, dim)


def call(kernel, out_shape, *args, flops=0, transcendentals=0):
    moved = sum(a.size * a.dtype.itemsize for a in args)
    moved += sum(o.size * o.dtype.itemsize for o in jax.tree.leaves(out_shape))
    return pl.pallas_call(
        kernel,
        out_shape=out_shape,
        compiler_params=pltpu.CompilerParams(vmem_limit_bytes=VMEM_LIMIT),
        cost_estimate=pl.CostEstimate(
            flops=flops, bytes_accessed=moved, transcendentals=transcendentals
        ),
    )(*args)


def shape(dims, dtype=BF16):
    return jax.ShapeDtypeStruct(tuple(dims), dtype)


def spread_kernel(owners, capacity, mark, place_ref, rows_ref, *out_refs):
    me = lax.axis_index("dp")
    place = place_ref[...]
    rows = rows_ref[...]
    count = rows.shape[0]
    for k in range(owners):
        first = (me ^ k) * capacity
        onehot = (iota((capacity, count), 0) + first == place).astype(F32)
        block = dot(onehot.astype(BF16), rows)
        if mark:
            filled = jnp.sum(onehot, axis=1, keepdims=True)
            block = block + (1.0 - filled) * EMPTY
        out_refs[k][...] = block.astype(BF16)


def lookup_kernel(owners, capacity, place_ref, out_ref):
    me = lax.axis_index("dp")
    count = place_ref.shape[1]
    column = jnp.broadcast_to(place_ref[...].astype(F32), (LANES, count)).T[:, 0:1].astype(jnp.int32)
    slot = iota((count, owners * capacity), 1)
    at = (me ^ (slot // capacity)) * capacity + slot % capacity
    out_ref[...] = (at == column).astype(F32).astype(BF16)


def forward_kernel(owners, capacity, *refs):
    blocks = refs[:owners]
    users_ref, w_ref = refs[owners : owners + 2]
    (
        place_ref, unplace_ref, act_ref, slope_ref, xhat_ref, xhat_t_ref, x_rstd_ref,
        weights_ref, tangent_ref, nhat_ref, a_rstd_ref, gated_t_ref, q_t_ref, att_ref,
    ) = refs[owners + 2 :]
    me = lax.axis_index("dp")
    count, width = xhat_ref.shape
    half = width // HEADS
    valid = [blocks[k][:, 0:LANES].astype(F32) != EMPTY for k in range(owners)]
    counts = [jnp.sum(v.astype(F32), axis=0, keepdims=True) for v in valid]
    source = iota((owners, LANES), 0) ^ me
    starts = jnp.zeros((owners, LANES), F32)
    for k in range(owners):
        starts = starts + jnp.where(source > (me ^ k), counts[k], 0.0)
    within = iota((capacity, LANES), 0).astype(F32)
    target = jnp.concatenate(
        [jnp.where(valid[k], starts[k : k + 1] + within, -1.0) for k in range(owners)], axis=0
    )
    target_t = target.T[0:1, :]
    slots = owners * capacity
    place = (iota((count, slots), 0) == target_t.astype(jnp.int32)).astype(F32).astype(BF16)
    place_ref[...] = place
    column = target[:, 0:1].astype(jnp.int32)
    unplace_ref[...] = (iota((slots, count), 1) == column).astype(F32).astype(BF16)
    received = jnp.concatenate([blocks[k][...] for k in range(owners)], axis=0)
    x = dot(place, received)
    center = x - jnp.mean(x, axis=1, keepdims=True)
    rstd = lax.rsqrt(jnp.mean(center * center, axis=1, keepdims=True) + EPSILON)
    xhat32 = center * rstd
    xhat = xhat32.astype(BF16)
    xhat_ref[...] = xhat
    xhat_t_ref[...] = xhat32.T.astype(BF16)
    x_rstd_ref[...] = jnp.broadcast_to(rstd, (count, LANES))
    for part in range(4):
        columns = slice(part * width, (part + 1) * width)
        pre = dot(xhat, w_ref[:, columns])
        sig = 0.5 * jnp.tanh(0.5 * pre) + 0.5
        act = pre * sig
        act_ref[:, columns] = act.astype(BF16)
        slope_ref[:, columns] = (sig + act * (1.0 - sig)).astype(BF16)
        if part == 2:
            q_t_ref[...] = act.T.astype(BF16)
    users = users_ref[...]
    users_column = jnp.broadcast_to(users.astype(F32), (LANES, count)).T[:, 0:1].astype(jnp.int32)
    scale = half ** (-0.5)
    lane = iota((BLOCK, LANES), 1)
    for i in range(count // BLOCK):
        low = max(0, i - LONGEST // BLOCK) * BLOCK
        high = (i + 1) * BLOCK
        span = high - low
        rows = slice(i * BLOCK, high)
        keep = (users_column[rows] == users[:, low:high]) & (
            iota((BLOCK, span), 1) + low <= iota((BLOCK, span), 0) + i * BLOCK
        )
        for pair in range(width // LANES):
            lanes = slice(pair * LANES, (pair + 1) * LANES)
            v = act_ref[low:high, width + lanes.start : width + lanes.stop]
            q = act_ref[rows, 2 * width + lanes.start : 2 * width + lanes.stop]
            k = act_ref[low:high, 3 * width + lanes.start : 3 * width + lanes.stop]
            attended = jnp.zeros((BLOCK, LANES), F32)
            for inner in range(LANES // half):
                mine = lane // half == inner
                score = dot_nt(jnp.where(mine, q, jnp.zeros_like(q)), k) * scale
                sig = 0.5 * jnp.tanh(0.5 * score) + 0.5
                value = score * sig
                weight = jnp.where(keep, value, 0.0).astype(BF16)
                tangent = jnp.where(keep, (sig + value * (1.0 - sig)) * scale, 0.0)
                head = pair * (LANES // half) + inner
                weights_ref[head, i, :, 0:span] = weight
                tangent_ref[head, i, :, 0:span] = tangent.astype(BF16)
                attended = jnp.where(mine, dot(weight, v), attended)
            att_ref[rows, lanes] = attended
    attended = att_ref[...]
    center = attended - jnp.mean(attended, axis=1, keepdims=True)
    rstd = lax.rsqrt(jnp.mean(center * center, axis=1, keepdims=True) + EPSILON)
    nhat = center * rstd
    nhat_ref[...] = nhat.astype(BF16)
    a_rstd_ref[...] = jnp.broadcast_to(rstd, (count, LANES))
    gated_t_ref[...] = (nhat * act_ref[:, 0:width].astype(F32)).T.astype(BF16)


def backward_kernel(owners, capacity, *refs):
    blocks = refs[:owners]
    (
        place_ref, unplace_ref, act_ref, slope_ref, xhat_ref, x_rstd_ref, weights_ref,
        tangent_ref, nhat_ref, a_rstd_ref, q_t_ref, w_ref, w_out_ref,
    ) = refs[owners : owners + 13]
    dy_ref, dpre_ref = refs[owners + 13 : owners + 15]
    out_refs = refs[owners + 15 : 2 * owners + 15]
    datt_ref, datt_t_ref, dkv_t_ref = refs[2 * owners + 15 :]
    count, width = xhat_ref.shape
    half = width // HEADS
    received = jnp.concatenate([blocks[k][...] for k in range(owners)], axis=0)
    dy32 = dot(place_ref[...], received)
    dy = dy32.astype(BF16)
    dy_ref[...] = dy
    dgated = dot_nt(dy, w_out_ref[...])
    nhat = nhat_ref[...].astype(F32)
    dpre_ref[:, 0:width] = (dgated * nhat * slope_ref[:, 0:width].astype(F32)).astype(BF16)
    dnhat = dgated * act_ref[:, 0:width].astype(F32)
    datt = a_rstd_ref[:, 0:1] * (
        dnhat
        - jnp.mean(dnhat, axis=1, keepdims=True)
        - nhat * jnp.mean(dnhat * nhat, axis=1, keepdims=True)
    )
    datt_ref[...] = datt.astype(BF16)
    datt_t_ref[...] = datt.T.astype(BF16)
    lane = iota((BLOCK, LANES), 1)
    steps = count // BLOCK
    for pair in range(width // LANES):
        lanes = slice(pair * LANES, (pair + 1) * LANES)
        dq = [jnp.zeros((BLOCK, LANES), F32) for _ in range(steps)]
        for inner in range(LANES // half):
            mine = lane // half == inner
            head = pair * (LANES // half) + inner
            own = slice(head * half, (head + 1) * half)
            dk_t = [None] * steps
            dv_t = [None] * steps
            for i in range(steps):
                start = max(0, i - LONGEST // BLOCK)
                low, high = start * BLOCK, (i + 1) * BLOCK
                span = high - low
                rows = slice(i * BLOCK, high)
                v = act_ref[low:high, width + lanes.start : width + lanes.stop]
                k = act_ref[low:high, 3 * width + lanes.start : 3 * width + lanes.stop]
                da = datt_ref[rows, lanes]
                dweight = dot_nt(jnp.where(mine, da, jnp.zeros_like(da)), v)
                dscore = (dweight * tangent_ref[head, i, :, 0:span].astype(F32)).astype(BF16)
                dq[i] = jnp.where(mine, dot(dscore, k), dq[i])
                add_k = dot(q_t_ref[own, rows], dscore)
                add_v = dot(datt_t_ref[own, rows], weights_ref[head, i, :, 0:span])
                for j in range(start, i + 1):
                    at = slice((j - start) * BLOCK, (j - start + 1) * BLOCK)
                    dk_t[j] = add_k[:, at] if dk_t[j] is None else dk_t[j] + add_k[:, at]
                    dv_t[j] = add_v[:, at] if dv_t[j] is None else dv_t[j] + add_v[:, at]
            for j in range(steps):
                at = slice(j * BLOCK, (j + 1) * BLOCK)
                dkv_t_ref[0, inner * half : (inner + 1) * half, at] = dv_t[j]
                dkv_t_ref[1, inner * half : (inner + 1) * half, at] = dk_t[j]
        for part, grad in (
            (1, dkv_t_ref[0].T),
            (2, jnp.concatenate(dq, axis=0)),
            (3, dkv_t_ref[1].T),
        ):
            columns = slice(part * width + lanes.start, part * width + lanes.stop)
            dpre_ref[:, columns] = (grad * slope_ref[:, columns].astype(F32)).astype(BF16)
    dxhat = dot_nt(dpre_ref[...], w_ref[...])
    xhat = xhat_ref[...].astype(F32)
    dx = dy32 + x_rstd_ref[:, 0:1] * (
        dxhat
        - jnp.mean(dxhat, axis=1, keepdims=True)
        - xhat * jnp.mean(dxhat * xhat, axis=1, keepdims=True)
    )
    dx = dx.astype(BF16)
    for k in range(owners):
        rows = slice(k * capacity, (k + 1) * capacity)
        out_refs[k][...] = dot(unplace_ref[rows, :], dx).astype(BF16)


def fold(piece):
    rows, columns = piece.shape
    if columns >= LANES:
        return jnp.concatenate(
            [piece[:, c : c + LANES] for c in range(0, columns, LANES)], axis=0
        )
    step = rows * columns // LANES
    return jnp.concatenate([piece[r : r + step] for r in range(0, rows, step)], axis=1)


def unfold(piece, rows, columns):
    if columns >= LANES:
        return jnp.concatenate(
            [piece[r : r + rows] for r in range(0, piece.shape[0], rows)], axis=1
        )
    return jnp.concatenate(
        [piece[:, c : c + columns] for c in range(0, LANES, columns)], axis=0
    )


def halves_first(index, size):
    return (index & 1) * (size // 2) + (index >> 1)


def weight_kernel(owners, groups, xhat_t_ref, dpre_ref, gated_t_ref, dy_ref, keep_ref, send_ref):
    me = lax.axis_index("dp")
    group = lax.axis_index("rep")
    width = xhat_t_ref.shape[0]
    part = width // groups
    in_grad = dot(xhat_t_ref[...], dpre_ref[...])
    out_grad = dot(gated_t_ref[...], dy_ref[...])
    in_cols = in_grad.shape[1] // owners
    out_cols = out_grad.shape[1] // owners
    in_rows = part * in_cols // LANES
    for r in range(groups):
        rows = slice(r * part, (r + 1) * part)
        relative = group ^ r
        for target, ref in ((0, keep_ref), (1, send_ref)):

            @pl.when((relative & 1) == target)
            def _():
                for d in range(owners):
                    at = halves_first(me ^ d, owners)
                    ref[relative >> 1, at, 0:in_rows, :] = fold(
                        in_grad[rows, d * in_cols : (d + 1) * in_cols]
                    ).astype(BF16)
                    ref[relative >> 1, at, in_rows:, :] = fold(
                        out_grad[rows, d * out_cols : (d + 1) * out_cols]
                    ).astype(BF16)


def add_kernel(kept_ref, got_ref, keep_ref, send_ref):
    half = kept_ref.shape[0] // 2
    send_ref[...] = (kept_ref[half:].astype(F32) + got_ref[half:].astype(F32)).astype(BF16)
    keep_ref[...] = (kept_ref[:half].astype(F32) + got_ref[:half].astype(F32)).astype(BF16)


def total_kernel(*refs):
    total = refs[0][...].astype(F32)
    for ref in refs[1:-1]:
        total = total + ref[...].astype(F32)
    refs[-1][...] = total.astype(BF16)


def result_kernel(groups, in_cols, out_cols, *refs):
    in_ref, out_ref = refs[groups:]
    group = lax.axis_index("rep")
    part = in_ref.shape[0] // groups
    in_rows = part * in_cols // LANES
    for k in range(groups):
        rows = pl.ds(pl.multiple_of((group ^ k) * part, part), part)
        piece = refs[k][...].astype(F32)
        in_ref[rows, :] = unfold(piece[:in_rows], part, in_cols)
        out_ref[rows, :] = unfold(piece[in_rows:], part, out_cols)


def collect_kernel(owners, *refs):
    lookup_ref, out_ref = refs[owners:]
    rows = jnp.concatenate([refs[k][...] for k in range(owners)], axis=0)
    out_ref[...] = dot(lookup_ref[...], rows).astype(BF16)


def swap(value, axis, distance):
    size = lax.axis_size(axis)
    return lax.ppermute(value, axis, [(i, i ^ distance) for i in range(size)])


def exchange(blocks):
    return [blocks[0]] + [swap(blocks[k], "dp", k) for k in range(1, len(blocks))]


def on_device(events, grad_out, w_uvqk, w_out, send_place, send_counts, user_ids):
    owners = lax.axis_size("dp")
    groups = lax.axis_size("rep")
    count, width = events.shape
    capacity = 2 * count // owners
    slots = owners * capacity
    spans = (LONGEST // BLOCK + 1) * BLOCK
    steps = count // BLOCK
    block_shapes = [shape((capacity, width))] * owners
    route = 2 * slots * count * width

    spread = functools.partial(spread_kernel, owners, capacity)
    x_blocks = call(functools.partial(spread, True), block_shapes, send_place, events, flops=route)
    dy_blocks = call(
        functools.partial(spread, False), block_shapes, send_place, grad_out, flops=route
    )
    lookup = call(
        functools.partial(lookup_kernel, owners, capacity), shape((count, slots)), send_place
    )
    x_blocks = exchange(x_blocks)
    dy_blocks = exchange(dy_blocks)
    square = shape((count, width))
    square_t = shape((width, count))
    wide = shape((count, 4 * width))
    column = shape((count, LANES), F32)
    scores = shape((HEADS, steps, BLOCK, spans))
    project = 2 * count * width * 4 * width
    attend = 2 * count * spans * width
    (
        place, unplace, act, slope, xhat, xhat_t, x_rstd,
        weights, tangent, nhat, a_rstd, gated_t, q_t, _,
    ) = call(
        functools.partial(forward_kernel, owners, capacity),
        [
            shape((count, slots)), shape((slots, count)), wide, wide, square, square_t, column,
            scores, scores, square, column, square_t, square_t, shape((count, width), F32),
        ],
        *x_blocks, user_ids, w_uvqk,
        flops=route + project + 2 * attend, transcendentals=HEADS * count * spans,
    )
    backward = functools.partial(backward_kernel, owners, capacity)
    moved = 24 * 1024 * 1024
    results = pl.pallas_call(
        backward,
        out_shape=[square, wide] + block_shapes,
        scratch_shapes=[
            pltpu.VMEM((count, width), BF16),
            pltpu.VMEM((width, count), BF16),
            pltpu.VMEM((2, LANES, count), F32),
        ],
        compiler_params=pltpu.CompilerParams(vmem_limit_bytes=VMEM_LIMIT),
        cost_estimate=pl.CostEstimate(
            flops=2 * route + project + 4 * attend, bytes_accessed=moved, transcendentals=0
        ),
    )(
        *dy_blocks, place, unplace, act, slope, xhat, x_rstd, weights, tangent, nhat, a_rstd,
        q_t, w_uvqk, w_out,
    )
    owned_dy, dpre = results[:2]
    back = exchange(results[2:])
    rows = 5 * width * width // (owners * groups * LANES)
    kept, sent = call(
        functools.partial(weight_kernel, owners, groups),
        [shape((groups // 2, owners, rows, LANES))] * 2,
        xhat_t, dpre, gated_t, owned_dy, flops=project + project // 4,
    )
    got = swap(sent, "rep", 1)
    distance = 2
    while distance < groups:
        half = kept.shape[0] // 2
        kept, sent = call(add_kernel, [shape((half,) + kept.shape[1:])] * 2, kept, got)
        got = swap(sent, "rep", distance)
        distance *= 2
    kept, got = kept[0], got[0]
    kept, sent = call(add_kernel, [shape((owners // 2,) + kept.shape[1:])] * 2, kept, got)
    got = swap(sent, "dp", 1)
    total = call(total_kernel, shape(kept.shape), kept, got)
    pieces = [total[0]] + [swap(total[k], "dp", 2 * k) for k in range(1, owners // 2)]
    own = call(total_kernel, shape((rows, LANES)), *pieces)
    shares = [own] + [swap(own, "rep", k) for k in range(1, groups)]
    in_cols = 4 * width // owners
    out_cols = width // owners
    share_in, share_out = call(
        functools.partial(result_kernel, groups, in_cols, out_cols),
        [shape((width, in_cols), F32), shape((width, out_cols), F32)],
        *shares,
    )
    grad_events = call(
        functools.partial(collect_kernel, owners), square, *back, lookup, flops=route
    )
    return (grad_events, share_in, share_out)


def solution(mesh):
    return jax.shard_map(
        on_device,
        mesh=mesh,
        in_specs=(
            P(("dp", "rep"), None),
            P(("dp", "rep"), None),
            P(),
            P(),
            P(("dp", "rep"), None),
            P(("dp", "rep"), None),
            P(("dp", "rep"), None),
        ),
        out_specs=(P(("dp", "rep"), None), P(None, "dp"), P(None, "dp")),
        check_vma=False,
    )
```

```python
import functools

import jax
import jax.numpy as jnp
from jax import lax
from jax.experimental import pallas as pl
from jax.experimental.pallas import tpu as pltpu
from jax.sharding import PartitionSpec as P

HEADS = 8
LONGEST = 256
EPSILON = 1e-05
EMPTY = 128.0
BLOCK = 128
QUERIES = 256
LANES = 128
F32 = jnp.float32
BF16 = jnp.bfloat16


def dot(a, b):
    return jnp.dot(a, b, preferred_element_type=F32)


def dot_nt(a, b):
    return lax.dot_general(a, b, (((1,), (1,)), ((), ())), preferred_element_type=F32)


def iota(shape, dim):
    return lax.broadcasted_iota(jnp.int32, shape, dim)


def call(kernel, out_shape, *args, flops=0, transcendentals=0, scratch=(), vmem=16):
    moved = sum(a.size * a.dtype.itemsize for a in args)
    moved += sum(o.size * o.dtype.itemsize for o in jax.tree.leaves(out_shape))
    return pl.pallas_call(
        kernel,
        out_shape=out_shape,
        scratch_shapes=scratch,
        compiler_params=pltpu.CompilerParams(vmem_limit_bytes=vmem * 1024 * 1024),
        cost_estimate=pl.CostEstimate(
            flops=flops, bytes_accessed=moved, transcendentals=transcendentals
        ),
    )(*args)


def shape(dims, dtype=BF16):
    return jax.ShapeDtypeStruct(tuple(dims), dtype)


def spread_kernel(owners, capacity, mark, place_ref, rows_ref, *out_refs):
    me = lax.axis_index("dp")
    place = place_ref[...]
    rows = rows_ref[...]
    count = rows.shape[0]
    for k in range(owners):
        first = (me ^ k) * capacity
        onehot = (iota((capacity, count), 0) + first == place).astype(F32)
        block = dot(onehot.astype(BF16), rows)
        if mark:
            filled = jnp.sum(onehot, axis=1, keepdims=True)
            block = block + (1.0 - filled) * EMPTY
        out_refs[k][...] = block.astype(BF16)


def lookup_kernel(place_ref, out_ref):
    count = place_ref.shape[1]
    column = jnp.broadcast_to(place_ref[...].astype(F32), (LANES, count)).T[:, 0:1].astype(jnp.int32)
    out_ref[...] = (iota(out_ref.shape, 1) == column).astype(F32).astype(BF16)


def key_range(i):
    return max(0, (i * QUERIES - LONGEST + 1) // QUERIES) * QUERIES, (i + 1) * QUERIES


def by_head(rows, lane, half):
    heads = range(LANES // half)
    return jnp.concatenate(
        [jnp.where(lane // half == h, rows, jnp.zeros_like(rows)) for h in heads], axis=0
    )


def own_head(rows, lane, half):
    total = rows[:QUERIES]
    for h in range(1, LANES // half):
        total = jnp.where(lane // half == h, rows[h * QUERIES : (h + 1) * QUERIES], total)
    return total


def forward_kernel(owners, capacity, *refs):
    blocks = refs[:owners]
    users_ref, w_ref = refs[owners : owners + 2]
    (
        place_ref, unplace_ref, act_ref, slope_ref, xhat_ref, xhat_t_ref, x_rstd_ref,
        weights_ref, tangent_ref, nhat_ref, a_rstd_ref, gated_t_ref, q_t_ref, att_ref,
    ) = refs[owners + 2 :]
    me = lax.axis_index("dp")
    count, width = xhat_ref.shape
    half = width // HEADS
    valid = [blocks[k][:, 0:LANES].astype(F32) != EMPTY for k in range(owners)]
    counts = [jnp.sum(v.astype(F32), axis=0, keepdims=True) for v in valid]
    source = iota((owners, LANES), 0) ^ me
    starts = jnp.zeros((owners, LANES), F32)
    for k in range(owners):
        starts = starts + jnp.where(source > (me ^ k), counts[k], 0.0)
    within = iota((capacity, LANES), 0).astype(F32)
    target = jnp.concatenate(
        [jnp.where(valid[k], starts[k : k + 1] + within, -1.0) for k in range(owners)], axis=0
    )
    target_t = target.T[0:1, :]
    slots = owners * capacity
    place = (iota((count, slots), 0) == target_t.astype(jnp.int32)).astype(F32).astype(BF16)
    place_ref[...] = place
    column = target[:, 0:1].astype(jnp.int32)
    unplace_ref[...] = (iota((slots, count), 1) == column).astype(F32).astype(BF16)
    received = jnp.concatenate([blocks[k][...] for k in range(owners)], axis=0)
    x = dot(place, received)
    center = x - jnp.mean(x, axis=1, keepdims=True)
    rstd = lax.rsqrt(jnp.mean(center * center, axis=1, keepdims=True) + EPSILON)
    xhat32 = center * rstd
    xhat = xhat32.astype(BF16)
    xhat_ref[...] = xhat
    xhat_t_ref[...] = xhat32.T.astype(BF16)
    x_rstd_ref[...] = jnp.broadcast_to(rstd, (count, LANES))
    for part in range(4):
        columns = slice(part * width, (part + 1) * width)
        pre = dot(xhat, w_ref[:, columns])
        sig = 0.5 * jnp.tanh(0.5 * pre) + 0.5
        act = pre * sig
        act_ref[:, columns] = act.astype(BF16)
        slope_ref[:, columns] = (sig + act * (1.0 - sig)).astype(BF16)
        if part == 2:
            q_t_ref[...] = act.T.astype(BF16)
    users = users_ref[...]
    users_column = jnp.broadcast_to(users.astype(F32), (LANES, count)).T[:, 0:1].astype(jnp.int32)
    scale = half ** (-0.5)
    lane = iota((QUERIES, LANES), 1)
    for i in range(count // QUERIES):
        low, high = key_range(i)
        rows = slice(i * QUERIES, high)
        keep = (users_column[rows] == users[:, low:high]) & (
            iota((QUERIES, high - low), 1) + low <= iota((QUERIES, high - low), 0) + i * QUERIES
        )
        for pair in range(width // LANES):
            lanes = slice(pair * LANES, (pair + 1) * LANES)
            v = act_ref[low:high, width + lanes.start : width + lanes.stop]
            q = act_ref[rows, 2 * width + lanes.start : 2 * width + lanes.stop]
            k = act_ref[low:high, 3 * width + lanes.start : 3 * width + lanes.stop]
            scores = dot_nt(by_head(q, lane, half), k)
            weights = []
            for inner in range(LANES // half):
                head = pair * (LANES // half) + inner
                for r in range(0, QUERIES, BLOCK):
                    for c in range(low, high, BLOCK):
                        at = (slice(r, r + BLOCK), slice(c - low, c - low + BLOCK))
                        first = i * QUERIES + r
                        if c > first or c + LONGEST < first:
                            weights_ref[(head, i) + at] = jnp.zeros((BLOCK, BLOCK), BF16)
                            tangent_ref[(head, i) + at] = jnp.zeros((BLOCK, BLOCK), BF16)
                            continue
                        score = scores[inner * QUERIES + r : inner * QUERIES + r + BLOCK, at[1]]
                        sig = 0.5 * jnp.tanh(score * (0.5 * scale)) + 0.5
                        value = score * scale * sig
                        slope = (sig + value * (1.0 - sig)) * scale
                        weights_ref[(head, i) + at] = jnp.where(keep[at], value, 0.0).astype(BF16)
                        tangent_ref[(head, i) + at] = jnp.where(keep[at], slope, 0.0).astype(BF16)
                weights.append(weights_ref[head, i, :, 0 : high - low])
            att_ref[rows, lanes] = own_head(dot(jnp.concatenate(weights, axis=0), v), lane, half)
    attended = att_ref[...]
    center = attended - jnp.mean(attended, axis=1, keepdims=True)
    rstd = lax.rsqrt(jnp.mean(center * center, axis=1, keepdims=True) + EPSILON)
    nhat = center * rstd
    nhat_ref[...] = nhat.astype(BF16)
    a_rstd_ref[...] = jnp.broadcast_to(rstd, (count, LANES))
    gated_t_ref[...] = (nhat * act_ref[:, 0:width].astype(F32)).T.astype(BF16)


def fold(piece):
    rows, columns = piece.shape
    if columns >= LANES:
        return jnp.concatenate(
            [piece[:, c : c + LANES] for c in range(0, columns, LANES)], axis=0
        )
    step = rows * columns // LANES
    return jnp.concatenate([piece[r : r + step] for r in range(0, rows, step)], axis=1)


def unfold(piece, rows, columns):
    if columns >= LANES:
        return jnp.concatenate(
            [piece[r : r + rows] for r in range(0, piece.shape[0], rows)], axis=1
        )
    return jnp.concatenate(
        [piece[:, c : c + columns] for c in range(0, LANES, columns)], axis=0
    )


def backward_kernel(owners, *refs):
    blocks = refs[:owners]
    (
        place_ref, act_ref, slope_ref, nhat_ref, a_rstd_ref, weights_ref, tangent_ref, q_t_ref,
        w_out_ref, dy_ref, dpre_ref, datt_ref, datt_t_ref, dkv_t_ref,
    ) = refs[owners:]
    count, width = dy_ref.shape
    half = width // HEADS
    received = jnp.concatenate([blocks[k][...] for k in range(owners)], axis=0)
    dy = dot(place_ref[...], received).astype(BF16)
    dy_ref[...] = dy
    dgated = dot_nt(dy, w_out_ref[...])
    nhat = nhat_ref[...].astype(F32)
    dpre_ref[:, 0:width] = (dgated * nhat * slope_ref[:, 0:width].astype(F32)).astype(BF16)
    dnhat = dgated * act_ref[:, 0:width].astype(F32)
    datt = a_rstd_ref[:, 0:1] * (
        dnhat
        - jnp.mean(dnhat, axis=1, keepdims=True)
        - nhat * jnp.mean(dnhat * nhat, axis=1, keepdims=True)
    )
    datt_ref[...] = datt.astype(BF16)
    datt_t_ref[...] = datt.T.astype(BF16)
    lane = iota((QUERIES, LANES), 1)
    steps = count // QUERIES
    heads = LANES // half
    for pair in range(width // LANES):
        lanes = slice(pair * LANES, (pair + 1) * LANES)
        dq = []
        dk_t = [[None] * steps for _ in range(heads)]
        dv_t = [[None] * steps for _ in range(heads)]
        for i in range(steps):
            low, high = key_range(i)
            rows = slice(i * QUERIES, high)
            v = act_ref[low:high, width + lanes.start : width + lanes.stop]
            k = act_ref[low:high, 3 * width + lanes.start : 3 * width + lanes.stop]
            dweight = dot_nt(by_head(datt_ref[rows, lanes], lane, half), v)
            dscore = []
            for inner in range(heads):
                head = pair * heads + inner
                own = slice(head * half, (head + 1) * half)
                tangent = tangent_ref[head, i, :, 0 : high - low].astype(F32)
                one = (dweight[inner * QUERIES : (inner + 1) * QUERIES] * tangent).astype(BF16)
                dscore.append(one)
                add_k = dot(q_t_ref[own, rows], one)
                add_v = dot(datt_t_ref[own, rows], weights_ref[head, i, :, 0 : high - low])
                for j in range(low // QUERIES, i + 1):
                    at = slice(j * QUERIES - low, (j + 1) * QUERIES - low)
                    for sums, add in ((dk_t[inner], add_k), (dv_t[inner], add_v)):
                        sums[j] = add[:, at] if sums[j] is None else sums[j] + add[:, at]
            dq.append(own_head(dot(jnp.concatenate(dscore, axis=0), k), lane, half))
        for inner in range(heads):
            for j in range(steps):
                at = slice(j * QUERIES, (j + 1) * QUERIES)
                dkv_t_ref[0, inner * half : (inner + 1) * half, at] = dv_t[inner][j]
                dkv_t_ref[1, inner * half : (inner + 1) * half, at] = dk_t[inner][j]
        for part, grad in (
            (1, dkv_t_ref[0].T),
            (2, jnp.concatenate(dq, axis=0)),
            (3, dkv_t_ref[1].T),
        ):
            columns = slice(part * width + lanes.start, part * width + lanes.stop)
            slope = slope_ref[:, columns].astype(F32)
            dpre_ref[:, columns] = (grad * slope).astype(BF16)


def input_kernel(
    owners, capacity, dpre_ref, w_ref, xhat_ref, x_rstd_ref, dy_ref, unplace_ref, out_ref
):
    me = lax.axis_index("dp")
    dxhat = dot_nt(dpre_ref[...], w_ref[...])
    xhat = xhat_ref[...].astype(F32)
    dx = dy_ref[...].astype(F32) + x_rstd_ref[:, 0:1] * (
        dxhat
        - jnp.mean(dxhat, axis=1, keepdims=True)
        - xhat * jnp.mean(dxhat * xhat, axis=1, keepdims=True)
    )
    rows = dot(unplace_ref[...], dx.astype(BF16)).astype(BF16)
    for k in range(owners):
        at = pl.ds(pl.multiple_of((me ^ k) * capacity, capacity), capacity)
        out_ref[at, :] = rows[k * capacity : (k + 1) * capacity]


def weight_kernel(owners, groups, xhat_t_ref, dpre_ref, gated_t_ref, dy_ref, kept_ref, sent_ref):
    me = lax.axis_index("dp")
    group = lax.axis_index("rep")
    in_grad = dot(xhat_t_ref[...], dpre_ref[...])
    out_grad = dot(gated_t_ref[...], dy_ref[...])
    in_cols = in_grad.shape[1] // owners
    out_cols = out_grad.shape[1] // owners
    part = in_grad.shape[0] // groups
    in_rows = part * in_cols // LANES
    for r in range(groups):
        rows = slice(r * part, (r + 1) * part)
        relative = group ^ r
        for target, ref in ((0, kept_ref), (1, sent_ref)):

            @pl.when((relative & 1) == target)
            def _():
                for d in range(owners):
                    side = (me ^ d) & 1
                    ref[relative >> 1, side, d // 2, 0:in_rows, :] = fold(
                        in_grad[rows, d * in_cols : (d + 1) * in_cols]
                    ).astype(BF16)
                    ref[relative >> 1, side, d // 2, in_rows:, :] = fold(
                        out_grad[rows, d * out_cols : (d + 1) * out_cols]
                    ).astype(BF16)


def added(first, second):
    return first.astype(F32) + second.astype(F32)


def core_sum_kernel(kept_ref, got_ref, a_kept_ref, a_sent_ref, b_kept_ref, b_sent_ref):
    half = kept_ref.shape[2] // 2
    a_sent_ref[...] = added(kept_ref[1, :, :half], got_ref[1, :, :half]).astype(BF16)
    b_sent_ref[...] = added(kept_ref[:, 1, half:], got_ref[:, 1, half:]).astype(BF16)
    a_kept_ref[...] = added(kept_ref[0, :, :half], got_ref[0, :, :half]).astype(BF16)
    b_kept_ref[...] = added(kept_ref[:, 0, half:], got_ref[:, 0, half:]).astype(BF16)


def side_sum_kernel(
    a_ref, a_got_ref, b_ref, b_got_ref, a_kept_ref, a_sent_ref, b_kept_ref, b_sent_ref
):
    a_sent_ref[...] = added(a_ref[1], a_got_ref[1]).astype(BF16)
    b_sent_ref[...] = added(b_ref[1], b_got_ref[1]).astype(BF16)
    a_kept_ref[...] = added(a_ref[0], a_got_ref[0]).astype(BF16)
    b_kept_ref[...] = added(b_ref[0], b_got_ref[0]).astype(BF16)


def plane_sum_kernel(a_ref, a_got_ref, b_ref, b_got_ref, *refs):
    outs, total_ref = refs[:-1], refs[-1]
    half = a_ref.shape[0]
    total_ref[:half] = added(a_ref[...], a_got_ref[...]).astype(BF16)
    total_ref[half:] = added(b_ref[...], b_got_ref[...]).astype(BF16)
    pair = lax.axis_index("dp") >> 1
    for k, ref in enumerate(outs):
        ref[...] = total_ref[pair ^ k]


def total_kernel(*refs):
    total = refs[0][...].astype(F32)
    for ref in refs[1:-1]:
        total = total + ref[...].astype(F32)
    refs[-1][...] = total.astype(BF16)


def result_kernel(groups, in_rows, *refs):
    in_ref, out_ref = refs[groups:]
    group = lax.axis_index("rep")
    part = in_ref.shape[0] // groups
    for k in range(groups):
        rows = pl.ds(pl.multiple_of((group ^ k) * part, part), part)
        piece = refs[k][...].astype(F32)
        in_ref[rows, :] = unfold(piece[:in_rows], part, in_ref.shape[1])
        out_ref[:, rows] = unfold(piece[in_rows:], part, out_ref.shape[0]).T


def collect_kernel(lookup_ref, rows_ref, out_ref):
    out_ref[...] = dot(lookup_ref[...], rows_ref[...]).astype(BF16)


def swap(value, axis, distance):
    size = lax.axis_size(axis)
    return lax.ppermute(value, axis, [(i, i ^ distance) for i in range(size)])


def exchange(blocks, after=None):
    got = [blocks[0]]
    for k in range(1, len(blocks)):
        block = blocks[k]
        if after is not None:
            block, after[k] = lax.optimization_barrier((block, after[k]))
        got.append(swap(block, "dp", k))
    return got


def ordered(value, *earlier):
    return lax.optimization_barrier((value,) + earlier)[0]


def on_device(events, grad_out, w_uvqk, w_out, send_place, send_counts, user_ids):
    owners = lax.axis_size("dp")
    groups = lax.axis_size("rep")
    count, width = events.shape
    capacity = 2 * count // owners
    slots = owners * capacity
    steps = count // QUERIES
    spans = max(high - low for low, high in map(key_range, range(steps)))
    block_shapes = [shape((capacity, width))] * owners
    route = 2 * slots * count * width
    square = shape((count, width))
    square_t = shape((width, count))
    wide = shape((count, 4 * width))
    column = shape((count, LANES), F32)
    scores = shape((HEADS, steps, QUERIES, spans))
    project = 2 * count * width * 4 * width
    attend = 2 * count * spans * width

    spread = functools.partial(spread_kernel, owners, capacity)
    x_blocks = call(functools.partial(spread, True), block_shapes, send_place, events, flops=route)
    dy_blocks = call(
        functools.partial(spread, False), block_shapes, send_place, grad_out, flops=route
    )
    lookup = call(lookup_kernel, shape((count, slots)), send_place)
    x_blocks = exchange(x_blocks)
    dy_blocks = exchange(dy_blocks, x_blocks)
    (
        place, unplace, act, slope, xhat, xhat_t, x_rstd,
        weights, tangent, nhat, a_rstd, gated_t, q_t,
    ) = call(
        functools.partial(forward_kernel, owners, capacity),
        [
            shape((count, slots)), shape((slots, count)), wide, wide, square, square_t, column,
            scores, scores, square, column, square_t, square_t,
        ],
        *x_blocks, user_ids, w_uvqk,
        flops=route + project + 2 * attend, transcendentals=HEADS * count * spans,
        scratch=[pltpu.VMEM((count, width), F32)], vmem=28,
    )
    owned_dy, dpre = call(
        functools.partial(backward_kernel, owners), [square, wide],
        *dy_blocks, place, act, slope, nhat, a_rstd, weights, tangent, q_t, w_out,
        flops=route + project // 4 + 4 * attend,
        scratch=[
            pltpu.VMEM((count, width), BF16),
            pltpu.VMEM((width, count), BF16),
            pltpu.VMEM((2, LANES, count), F32),
        ],
        vmem=28,
    )
    pairs = owners // 2
    in_rows = width // groups * (4 * width // owners) // LANES
    rows = in_rows + width // groups * (width // owners) // LANES
    kept, sent = call(
        functools.partial(weight_kernel, owners, groups),
        [shape((2, 2, pairs, rows, LANES))] * 2,
        xhat_t, dpre, gated_t, owned_dy, flops=project + project // 4,
    )
    back = call(
        functools.partial(input_kernel, owners, capacity), shape((slots, width)),
        ordered(dpre, sent), w_uvqk, xhat, x_rstd, owned_dy, unplace, flops=project + route,
    )
    a_kept, a_sent, b_kept, b_sent = call(
        core_sum_kernel, [shape((2, pairs // 2, rows, LANES))] * 4, kept, swap(sent, "rep", 1)
    )
    back = ordered(back, a_sent, b_sent)
    back = lax.all_to_all(back, "dp", split_axis=0, concat_axis=0, tiled=True)
    a_kept, a_sent, b_kept, b_sent = call(
        side_sum_kernel, [shape((pairs // 2, rows, LANES))] * 4,
        a_kept, swap(a_sent, "rep", 2), b_kept, swap(b_sent, "dp", 1),
    )
    pieces = call(
        plane_sum_kernel, [shape((rows, LANES))] * pairs,
        a_kept, swap(a_sent, "dp", 1), b_kept, swap(b_sent, "rep", 2),
        scratch=[pltpu.VMEM((pairs, rows, LANES), BF16)],
    )
    pieces = [pieces[0]] + [swap(pieces[k], "dp", 2 * k) for k in range(1, pairs)]
    own = call(total_kernel, shape((rows, LANES)), *pieces)
    far = swap(own, "rep", 2)
    shares = [own, swap(own, "rep", 1), far, swap(far, "rep", 1)]
    share_in, share_out = call(
        functools.partial(result_kernel, groups, in_rows),
        [shape((width, 4 * width // owners), F32), shape((width // owners, width), F32)],
        *shares,
    )
    grad_events = call(collect_kernel, square, lookup, back, flops=route)
    return (grad_events, share_in, share_out.T)


def solution(mesh):
    return jax.shard_map(
        on_device,
        mesh=mesh,
        in_specs=(
            P(("dp", "rep"), None),
            P(("dp", "rep"), None),
            P(),
            P(),
            P(("dp", "rep"), None),
            P(("dp", "rep"), None),
            P(("dp", "rep"), None),
        ),
        out_specs=(P(("dp", "rep"), None), P(None, "dp"), P(None, "dp")),
        check_vma=False,
    )
```

```python
import functools

import jax
import jax.numpy as jnp
from jax import lax
from jax.experimental import pallas as pl
from jax.experimental.pallas import tpu as pltpu
from jax.sharding import PartitionSpec as P

HEADS = 8
LONGEST = 256
EPSILON = 1e-05
EMPTY = 128.0
BLOCK = 128
QUERIES = 256
LANES = 128
F32 = jnp.float32
WAITING = 3 * 10**9
BF16 = jnp.bfloat16


def dot(a, b):
    return jnp.dot(a, b, preferred_element_type=F32)


def dot_nt(a, b):
    return lax.dot_general(a, b, (((1,), (1,)), ((), ())), preferred_element_type=F32)


def iota(shape, dim):
    return lax.broadcasted_iota(jnp.int32, shape, dim)


def call(kernel, out_shape, *args, flops=0, transcendentals=0, scratch=(), vmem=16):
    moved = sum(a.size * a.dtype.itemsize for a in args)
    moved += sum(o.size * o.dtype.itemsize for o in jax.tree.leaves(out_shape))
    return pl.pallas_call(
        kernel,
        out_shape=out_shape,
        scratch_shapes=scratch,
        compiler_params=pltpu.CompilerParams(vmem_limit_bytes=vmem * 1024 * 1024),
        cost_estimate=pl.CostEstimate(
            flops=flops, bytes_accessed=moved, transcendentals=transcendentals
        ),
    )(*args)


def shape(dims, dtype=BF16):
    return jax.ShapeDtypeStruct(tuple(dims), dtype)


def far_first(owners):
    return [0, *range(owners // 2, owners)]


def selection(first, capacity, place):
    return (iota((capacity, place.shape[1]), 0) + first == place).astype(F32)


def selected(onehot, rows):
    return dot(onehot.astype(BF16), rows).astype(BF16)


def marked(onehot, rows):
    block = dot(onehot.astype(BF16), rows)
    return (block + (1.0 - jnp.sum(onehot, axis=1, keepdims=True)) * EMPTY).astype(BF16)


def spread_x_kernel(owners, capacity, place_ref, x_ref, *out_refs):
    me = lax.axis_index("dp")
    for k, ref in zip(far_first(owners), out_refs):
        ref[...] = marked(selection((me ^ k) * capacity, capacity, place_ref[...]), x_ref[...])


def spread_dy_kernel(owners, capacity, place_ref, x_ref, dy_ref, *out_refs):
    me = lax.axis_index("dp")
    for k, ref in enumerate(out_refs):
        onehot = selection((me ^ k) * capacity, capacity, place_ref[...])
        if 0 < k < owners // 2:
            ref[:capacity] = marked(onehot, x_ref[...])
        ref[-capacity:] = selected(onehot, dy_ref[...])


def lookup_kernel(place_ref, out_ref):
    count = place_ref.shape[1]
    column = jnp.broadcast_to(place_ref[...].astype(F32), (LANES, count)).T[:, 0:1].astype(jnp.int32)
    out_ref[...] = (iota(out_ref.shape, 1) == column).astype(F32).astype(BF16)


def key_range(i):
    return max(0, (i * QUERIES - LONGEST + 1) // QUERIES) * QUERIES, (i + 1) * QUERIES


def by_head(rows, lane, half):
    heads = range(LANES // half)
    return jnp.concatenate(
        [jnp.where(lane // half == h, rows, jnp.zeros_like(rows)) for h in heads], axis=0
    )


def own_head(rows, lane, half):
    total = rows[:QUERIES]
    for h in range(1, LANES // half):
        total = jnp.where(lane // half == h, rows[h * QUERIES : (h + 1) * QUERIES], total)
    return total


def forward_kernel(owners, capacity, *refs):
    blocks = refs[:owners]
    users_ref, w_ref = refs[owners : owners + 2]
    (
        place_ref, unplace_ref, act_ref, slope_ref, xhat_ref, xhat_t_ref, x_rstd_ref,
        weights_ref, tangent_ref, nhat_ref, a_rstd_ref, gated_t_ref, q_t_ref, att_ref,
    ) = refs[owners + 2 :]
    me = lax.axis_index("dp")
    count, width = xhat_ref.shape
    half = width // HEADS
    valid = [blocks[k][:capacity, 0:LANES].astype(F32) != EMPTY for k in range(owners)]
    counts = [jnp.sum(v.astype(F32), axis=0, keepdims=True) for v in valid]
    source = iota((owners, LANES), 0) ^ me
    starts = jnp.zeros((owners, LANES), F32)
    for k in range(owners):
        starts = starts + jnp.where(source > (me ^ k), counts[k], 0.0)
    within = iota((capacity, LANES), 0).astype(F32)
    target = jnp.concatenate(
        [jnp.where(valid[k], starts[k : k + 1] + within, -1.0) for k in range(owners)], axis=0
    )
    target_t = target.T[0:1, :]
    slots = owners * capacity
    place = (iota((count, slots), 0) == target_t.astype(jnp.int32)).astype(F32).astype(BF16)
    place_ref[...] = place
    column = target[:, 0:1].astype(jnp.int32)
    unplace_ref[...] = (iota((slots, count), 1) == column).astype(F32).astype(BF16)
    received = jnp.concatenate([blocks[k][:capacity] for k in range(owners)], axis=0)
    x = dot(place, received)
    center = x - jnp.mean(x, axis=1, keepdims=True)
    rstd = lax.rsqrt(jnp.mean(center * center, axis=1, keepdims=True) + EPSILON)
    xhat32 = center * rstd
    xhat = xhat32.astype(BF16)
    xhat_ref[...] = xhat
    xhat_t_ref[...] = xhat32.T.astype(BF16)
    x_rstd_ref[...] = jnp.broadcast_to(rstd, (count, LANES))
    for part in range(4):
        columns = slice(part * width, (part + 1) * width)
        pre = dot(xhat, w_ref[:, columns])
        sig = 0.5 * jnp.tanh(0.5 * pre) + 0.5
        act = pre * sig
        act_ref[:, columns] = act.astype(BF16)
        slope_ref[:, columns] = (sig + act * (1.0 - sig)).astype(BF16)
        if part == 2:
            q_t_ref[...] = act.T.astype(BF16)
    users = users_ref[...]
    users_column = jnp.broadcast_to(users.astype(F32), (LANES, count)).T[:, 0:1].astype(jnp.int32)
    scale = half ** (-0.5)
    lane = iota((QUERIES, LANES), 1)
    for i in range(count // QUERIES):
        low, high = key_range(i)
        rows = slice(i * QUERIES, high)
        keep = (users_column[rows] == users[:, low:high]) & (
            iota((QUERIES, high - low), 1) + low <= iota((QUERIES, high - low), 0) + i * QUERIES
        )
        for pair in range(width // LANES):
            lanes = slice(pair * LANES, (pair + 1) * LANES)
            v = act_ref[low:high, width + lanes.start : width + lanes.stop]
            q = act_ref[rows, 2 * width + lanes.start : 2 * width + lanes.stop]
            k = act_ref[low:high, 3 * width + lanes.start : 3 * width + lanes.stop]
            scores = dot_nt(by_head(q, lane, half), k)
            weights = []
            for inner in range(LANES // half):
                head = pair * (LANES // half) + inner
                for r in range(0, QUERIES, BLOCK):
                    for c in range(low, high, BLOCK):
                        at = (slice(r, r + BLOCK), slice(c - low, c - low + BLOCK))
                        first = i * QUERIES + r
                        if c > first or c + LONGEST < first:
                            weights_ref[(head, i) + at] = jnp.zeros((BLOCK, BLOCK), BF16)
                            tangent_ref[(head, i) + at] = jnp.zeros((BLOCK, BLOCK), BF16)
                            continue
                        score = scores[inner * QUERIES + r : inner * QUERIES + r + BLOCK, at[1]]
                        sig = 0.5 * jnp.tanh(score * (0.5 * scale)) + 0.5
                        value = score * scale * sig
                        slope = (sig + value * (1.0 - sig)) * scale
                        weights_ref[(head, i) + at] = jnp.where(keep[at], value, 0.0).astype(BF16)
                        tangent_ref[(head, i) + at] = jnp.where(keep[at], slope, 0.0).astype(BF16)
                weights.append(weights_ref[head, i, :, 0 : high - low])
            att_ref[rows, lanes] = own_head(dot(jnp.concatenate(weights, axis=0), v), lane, half)
    attended = att_ref[...]
    center = attended - jnp.mean(attended, axis=1, keepdims=True)
    rstd = lax.rsqrt(jnp.mean(center * center, axis=1, keepdims=True) + EPSILON)
    nhat = center * rstd
    nhat_ref[...] = nhat.astype(BF16)
    a_rstd_ref[...] = jnp.broadcast_to(rstd, (count, LANES))
    gated_t_ref[...] = (nhat * act_ref[:, 0:width].astype(F32)).T.astype(BF16)


def fold(piece):
    rows, columns = piece.shape
    if columns >= LANES:
        return jnp.concatenate(
            [piece[:, c : c + LANES] for c in range(0, columns, LANES)], axis=0
        )
    step = rows * columns // LANES
    return jnp.concatenate([piece[r : r + step] for r in range(0, rows, step)], axis=1)


def unfold(piece, rows, columns):
    if columns >= LANES:
        return jnp.concatenate(
            [piece[r : r + rows] for r in range(0, piece.shape[0], rows)], axis=1
        )
    return jnp.concatenate(
        [piece[:, c : c + columns] for c in range(0, LANES, columns)], axis=0
    )


def attend_backward(
    pairs, act_ref, slope_ref, weights_ref, tangent_ref, q_t_ref, datt_ref, datt_t_ref,
    dpre_ref, dkv_t_ref,
):
    count, width = datt_ref.shape
    half = width // HEADS
    lane = iota((QUERIES, LANES), 1)
    steps = count // QUERIES
    heads = LANES // half
    for pair in pairs:
        lanes = slice(pair * LANES, (pair + 1) * LANES)
        dq = []
        dk_t = [[None] * steps for _ in range(heads)]
        dv_t = [[None] * steps for _ in range(heads)]
        for i in range(steps):
            low, high = key_range(i)
            rows = slice(i * QUERIES, high)
            v = act_ref[low:high, width + lanes.start : width + lanes.stop]
            k = act_ref[low:high, 3 * width + lanes.start : 3 * width + lanes.stop]
            dweight = dot_nt(by_head(datt_ref[rows, lanes], lane, half), v)
            dscore = []
            for inner in range(heads):
                head = pair * heads + inner
                own = slice(head * half, (head + 1) * half)
                tangent = tangent_ref[head, i, :, 0 : high - low].astype(F32)
                one = (dweight[inner * QUERIES : (inner + 1) * QUERIES] * tangent).astype(BF16)
                dscore.append(one)
                add_k = dot(q_t_ref[own, rows], one)
                add_v = dot(datt_t_ref[own, rows], weights_ref[head, i, :, 0 : high - low])
                for j in range(low // QUERIES, i + 1):
                    at = slice(j * QUERIES - low, (j + 1) * QUERIES - low)
                    for sums, add in ((dk_t[inner], add_k), (dv_t[inner], add_v)):
                        sums[j] = add[:, at] if sums[j] is None else sums[j] + add[:, at]
            dq.append(own_head(dot(jnp.concatenate(dscore, axis=0), k), lane, half))
        for inner in range(heads):
            for j in range(steps):
                at = slice(j * QUERIES, (j + 1) * QUERIES)
                dkv_t_ref[0, inner * half : (inner + 1) * half, at] = dv_t[inner][j]
                dkv_t_ref[1, inner * half : (inner + 1) * half, at] = dk_t[inner][j]
        for part, grad in (
            (1, dkv_t_ref[0].T),
            (2, jnp.concatenate(dq, axis=0)),
            (3, dkv_t_ref[1].T),
        ):
            columns = slice(part * width + lanes.start, part * width + lanes.stop)
            slope = slope_ref[:, columns].astype(F32)
            dpre_ref[:, columns] = (grad * slope).astype(BF16)


def cotangent_kernel(owners, capacity, *refs):
    blocks = refs[:owners]
    (
        place_ref, nhat_ref, a_rstd_ref, w_out_ref, act_ref, slope_ref,
        dy_ref, dpre_ref, datt_ref, datt_t_ref,
    ) = refs[owners:]
    width = dy_ref.shape[1]
    received = jnp.concatenate([blocks[k][-capacity:] for k in range(owners)], axis=0)
    dy = dot(place_ref[...], received).astype(BF16)
    dy_ref[...] = dy
    dgated = dot_nt(dy, w_out_ref[...])
    nhat = nhat_ref[...].astype(F32)
    dpre_ref[...] = (dgated * nhat * slope_ref[:, 0:width].astype(F32)).astype(BF16)
    dnhat = dgated * act_ref[:, 0:width].astype(F32)
    datt = a_rstd_ref[:, 0:1] * (
        dnhat
        - jnp.mean(dnhat, axis=1, keepdims=True)
        - nhat * jnp.mean(dnhat * nhat, axis=1, keepdims=True)
    )
    datt_ref[...] = datt.astype(BF16)
    datt_t_ref[...] = datt.T.astype(BF16)


def attention_kernel(dpre_u_ref, *refs):
    dpre_ref = refs[7]
    width = dpre_u_ref.shape[1]
    dpre_ref[:, 0:width] = dpre_u_ref[...]
    attend_backward(range(width // LANES), *refs)


def input_kernel(dpre_ref, w_ref, xhat_ref, x_rstd_ref, dy_ref, dx_ref):
    dxhat = dot_nt(dpre_ref[...], w_ref[...])
    xhat = xhat_ref[...].astype(F32)
    dx = dy_ref[...].astype(F32) + x_rstd_ref[:, 0:1] * (
        dxhat
        - jnp.mean(dxhat, axis=1, keepdims=True)
        - xhat * jnp.mean(dxhat * xhat, axis=1, keepdims=True)
    )
    dx_ref[...] = dx.astype(BF16)


def return_kernel(owners, capacity, dx_ref, unplace_ref, out_ref):
    me = lax.axis_index("dp")
    rows = dot(unplace_ref[...], dx_ref[...]).astype(BF16)
    for k in range(owners):
        at = pl.ds(pl.multiple_of((me ^ k) * capacity, capacity), capacity)
        out_ref[at, :] = rows[k * capacity : (k + 1) * capacity]


def term_rows(owners, groups, width):
    in_rows = width // groups * (4 * width // owners) // LANES
    return in_rows, width // groups * (width // owners) // LANES


def store_terms(grads, kept_ref, sent_ref, groups):
    group = lax.axis_index("rep")
    for r in range(groups):
        relative = group ^ r
        for target, ref in ((0, kept_ref), (1, sent_ref)):

            @pl.when((relative & 1) == target)
            def _():
                at = 0
                for grad in grads:
                    part = grad.shape[0] // groups
                    piece = fold(grad[r * part : (r + 1) * part]).astype(BF16)
                    ref[relative >> 1, at : at + piece.shape[0], :] = piece
                    at += piece.shape[0]


def columns_of(grad, owners_in):
    step = grad.shape[1] // owners_in
    return [grad[:, c : c + step] for c in range(0, grad.shape[1], step)]


def early_weight_kernel(
    owners, groups, xhat_t_ref, dpre_ref, gated_t_ref, dy_ref, kept_ref, sent_ref
):
    grads = columns_of(dot(xhat_t_ref[...], dpre_ref[...]), owners // 4)
    grads += columns_of(dot(gated_t_ref[...], dy_ref[...]), owners)
    store_terms(grads, kept_ref, sent_ref, groups)


def late_weight_kernel(owners, groups, xhat_t_ref, dpre_ref, kept_ref, sent_ref):
    width = xhat_t_ref.shape[0]
    grads = columns_of(dot(xhat_t_ref[...], dpre_ref[:, width:]), owners - owners // 4)
    store_terms(grads, kept_ref, sent_ref, groups)


def added(first, second):
    return first.astype(F32) + second.astype(F32)


def core_sum_kernel(kept_ref, got_ref, out_kept_ref, out_sent_ref):
    out_sent_ref[...] = added(kept_ref[1], got_ref[1]).astype(BF16)
    out_kept_ref[...] = added(kept_ref[0], got_ref[0]).astype(BF16)


def side_sum_kernel(owners, step, kept_ref, got_ref, out_kept_ref, out_sent_ref):
    me = lax.axis_index("dp")
    first = owners - kept_ref.shape[1] // step
    for d in range(first, owners):
        rows = slice((d - first) * step, (d - first + 1) * step)
        at = (d - first) // 2 * step
        term = added(kept_ref[:, rows, :], got_ref[:, rows, :]).astype(BF16)
        for target, ref in ((0, out_kept_ref), (1, out_sent_ref)):

            @pl.when(((me ^ d) & 1) == target)
            def _():
                ref[:, at : at + step, :] = term


def split_pairs(owners, sizes, first_ref, second_ref, kept_ref, sent_ref):
    me = lax.axis_index("dp")
    at = 0
    for number, step in sizes:
        base = at // 2
        for d in range(number):
            rows = slice(at, at + step)
            term = added(first_ref[rows, :], second_ref[rows, :]).astype(BF16)
            for target, ref in ((0, kept_ref), (1, sent_ref)):

                @pl.when(((me ^ d) & 1) == target)
                def _():
                    ref[base + d // 2 * step : base + (d // 2 + 1) * step, :] = term

            at += step


def plane_sum_kernel(owners, in_rows, out_rows, *refs):
    early_ref, early_got_ref, late_ref, late_got_ref = refs[:4]
    outs, total_ref = refs[4:-1], refs[-1]
    early = early_ref.shape[0]
    total_ref[:early] = added(early_ref[...], early_got_ref[...]).astype(BF16)
    total_ref[early:] = added(late_ref[...], late_got_ref[...]).astype(BF16)
    here = lax.axis_index("dp") >> 1
    quarter = owners // 8 * in_rows
    for k, ref in enumerate(outs):
        pair = here ^ k
        first = pair * in_rows
        first = jnp.where(first < quarter, first, first - quarter + early)
        ref[0:in_rows, :] = total_ref[pl.ds(pl.multiple_of(first, in_rows), in_rows), :]
        first = quarter + pair * out_rows
        ref[in_rows:, :] = total_ref[pl.ds(pl.multiple_of(first, out_rows), out_rows), :]


def total_kernel(*refs):
    total = refs[0][...].astype(F32)
    for ref in refs[1:-1]:
        total = total + ref[...].astype(F32)
    refs[-1][...] = total.astype(BF16)


def result_kernel(groups, in_rows, *refs):
    in_ref, out_ref = refs[groups:]
    group = lax.axis_index("rep")
    part = in_ref.shape[0] // groups
    for k in range(groups):
        rows = pl.ds(pl.multiple_of((group ^ k) * part, part), part)
        piece = refs[k][...].astype(F32)
        in_ref[rows, :] = unfold(piece[:in_rows], part, in_ref.shape[1])
        out_ref[:, rows] = unfold(piece[in_rows:], part, out_ref.shape[0]).T


def collect_kernel(lookup_ref, rows_ref, out_ref):
    out_ref[...] = dot(lookup_ref[...], rows_ref[...]).astype(BF16)


def swap(value, axis, distance):
    size = lax.axis_size(axis)
    return lax.ppermute(value, axis, [(i, i ^ distance) for i in range(size)])


def ordered(value, *earlier):
    return lax.optimization_barrier((value,) + earlier)[0]


def exchange(far_x, blocks):
    owners = len(blocks)
    got_x, got = list(blocks), list(blocks)
    for k, block in zip(far_first(owners), far_x):
        got_x[k] = swap(block, "dp", k) if k else block
    for k in range(1, owners):
        if k < owners // 2:
            got_x[k] = got[k] = swap(blocks[k], "dp", k)
        else:
            got[k] = swap(ordered(blocks[k], got_x[k]), "dp", k)
    return got_x, got


def on_device(events, grad_out, w_uvqk, w_out, send_place, send_counts, user_ids):
    owners = lax.axis_size("dp")
    groups = lax.axis_size("rep")
    count, width = events.shape
    capacity = 2 * count // owners
    slots = owners * capacity
    steps = count // QUERIES
    spans = max(high - low for low, high in map(key_range, range(steps)))
    route = 2 * slots * count * width
    square = shape((count, width))
    square_t = shape((width, count))
    wide = shape((count, 4 * width))
    column = shape((count, LANES), F32)
    scores = shape((HEADS, steps, QUERIES, spans))
    project = 2 * count * width * 4 * width
    attend = 2 * count * spans * width

    far_x = call(
        functools.partial(spread_x_kernel, owners, capacity),
        [shape((capacity, width))] * (owners // 2 + 1), send_place, events, flops=route // 2,
    )
    blocks = call(
        functools.partial(spread_dy_kernel, owners, capacity),
        [
            shape(((2 if 0 < k < owners // 2 else 1) * capacity, width))
            for k in range(owners)
        ],
        send_place, events, grad_out, flops=route,
    )
    lookup = call(lookup_kernel, shape((count, slots)), send_place)
    x_blocks, dy_blocks = exchange(far_x, blocks)
    (
        place, unplace, act, slope, xhat, xhat_t, x_rstd,
        weights, tangent, nhat, a_rstd, gated_t, q_t,
    ) = call(
        functools.partial(forward_kernel, owners, capacity),
        [
            shape((count, slots)), shape((slots, count)), wide, wide, square, square_t, column,
            scores, scores, square, column, square_t, square_t,
        ],
        *x_blocks, user_ids, w_uvqk,
        flops=route + project + 2 * attend, transcendentals=HEADS * count * spans,
        scratch=[pltpu.VMEM((count, width), F32)], vmem=28,
    )
    owned_dy, dpre_u, datt, datt_t = call(
        functools.partial(cotangent_kernel, owners, capacity),
        [square, square, square, square_t],
        *dy_blocks, place, nhat, a_rstd, w_out, act, slope, flops=route + project // 4,
    )
    in_rows, out_rows = term_rows(owners, groups, width)
    early_sizes = ((owners // 4, in_rows), (owners, out_rows))
    late_sizes = ((owners - owners // 4, in_rows),)
    early, late = (sum(n * rows for n, rows in sizes) for sizes in (early_sizes, late_sizes))
    early_kept, early_sent = call(
        functools.partial(early_weight_kernel, owners, groups),
        [shape((2, early, LANES))] * 2, xhat_t, dpre_u, gated_t, owned_dy, flops=project // 2,
    )
    dpre = call(
        attention_kernel, wide,
        dpre_u, act, slope, weights, tangent, q_t, ordered(datt, early_sent), datt_t,
        flops=4 * attend, scratch=[pltpu.VMEM((2, LANES, count), F32)], vmem=28,
    )
    early_kept, early_sent = call(
        core_sum_kernel, [shape((early, LANES))] * 2, early_kept, swap(early_sent, "rep", 1)
    )
    early_got = swap(early_sent, "rep", 2)
    late_kept, late_sent = call(
        functools.partial(late_weight_kernel, owners, groups),
        [shape((2, late, LANES))] * 2, xhat_t, ordered(dpre, early_sent), flops=project,
    )
    dx = call(
        input_kernel, square, ordered(dpre, late_sent), w_uvqk, xhat, x_rstd, owned_dy,
        flops=project,
    )
    late_kept, late_sent = call(
        functools.partial(side_sum_kernel, owners, in_rows), [shape((2, late // 2, LANES))] * 2,
        late_kept, swap(late_sent, "rep", 1),
    )
    back = call(
        functools.partial(return_kernel, owners, capacity), shape((slots, width)),
        ordered(dx, late_sent), unplace, flops=route,
    )
    late_got = swap(late_sent, "dp", 1)
    back = lax.all_to_all(back, "dp", split_axis=0, concat_axis=0, tiled=True)
    early_kept, early_sent = call(
        functools.partial(split_pairs, owners, early_sizes), [shape((early // 2, LANES))] * 2,
        early_kept, early_got, flops=WAITING,
    )
    late_kept, late_sent = call(
        core_sum_kernel, [shape((late // 2, LANES))] * 2, late_kept, late_got, flops=WAITING,
    )
    pairs = owners // 2
    rows = in_rows + out_rows
    pieces = call(
        functools.partial(plane_sum_kernel, owners, in_rows, out_rows),
        [shape((rows, LANES))] * pairs,
        early_kept, swap(early_sent, "dp", 1), late_kept, swap(late_sent, "rep", 2),
        flops=WAITING, scratch=[pltpu.VMEM(((early + late) // 2, LANES), BF16)],
    )
    pieces = [pieces[0]] + [swap(pieces[k], "dp", 2 * k) for k in range(1, pairs)]
    own = call(total_kernel, shape((rows, LANES)), *pieces, flops=WAITING)
    far = swap(own, "rep", 2)
    shares = [own, swap(own, "rep", 1), far, swap(far, "rep", 1)]
    grad_events = call(collect_kernel, square, lookup, back, flops=route)
    shares[0] = ordered(own, grad_events)
    share_in, share_out = call(
        functools.partial(result_kernel, groups, in_rows),
        [shape((width, 4 * width // owners), F32), shape((width // owners, width), F32)],
        *shares, flops=WAITING,
    )
    return (grad_events, share_in, share_out.T)


def solution(mesh):
    return jax.shard_map(
        on_device,
        mesh=mesh,
        in_specs=(
            P(("dp", "rep"), None),
            P(("dp", "rep"), None),
            P(),
            P(),
            P(("dp", "rep"), None),
            P(("dp", "rep"), None),
            P(("dp", "rep"), None),
        ),
        out_specs=(P(("dp", "rep"), None), P(None, "dp"), P(None, "dp")),
        check_vma=False,
    )
```

```python
import functools

import jax
import jax.numpy as jnp
from jax import lax
from jax.experimental import pallas as pl
from jax.experimental.pallas import tpu as pltpu
from jax.sharding import PartitionSpec as P

HEADS = 8
LONGEST = 256
EPSILON = 1e-05
EMPTY = 128.0
BLOCK = 128
QUERIES = 256
LANES = 128
F32 = jnp.float32
WAITING = 3 * 10**9
BF16 = jnp.bfloat16


def dot(a, b):
    return jnp.dot(a, b, preferred_element_type=F32)


def dot_nt(a, b):
    return lax.dot_general(a, b, (((1,), (1,)), ((), ())), preferred_element_type=F32)


def iota(shape, dim):
    return lax.broadcasted_iota(jnp.int32, shape, dim)


def call(kernel, out_shape, *args, flops=0, transcendentals=0, scratch=(), vmem=16):
    moved = sum(a.size * a.dtype.itemsize for a in args)
    moved += sum(o.size * o.dtype.itemsize for o in jax.tree.leaves(out_shape))
    return pl.pallas_call(
        kernel,
        out_shape=out_shape,
        scratch_shapes=scratch,
        compiler_params=pltpu.CompilerParams(vmem_limit_bytes=vmem * 1024 * 1024),
        cost_estimate=pl.CostEstimate(
            flops=flops, bytes_accessed=moved, transcendentals=transcendentals
        ),
    )(*args)


def shape(dims, dtype=BF16):
    return jax.ShapeDtypeStruct(tuple(dims), dtype)


def far_first(owners):
    return [0, *range(owners // 2, owners)]


def selection(first, capacity, place):
    return (iota((capacity, place.shape[1]), 0) + first == place).astype(F32)


def selected(onehot, rows):
    return dot(onehot.astype(BF16), rows).astype(BF16)


def marked(onehot, rows):
    block = dot(onehot.astype(BF16), rows)
    return (block + (1.0 - jnp.sum(onehot, axis=1, keepdims=True)) * EMPTY).astype(BF16)


def spread_x_kernel(owners, capacity, place_ref, x_ref, *out_refs):
    me = lax.axis_index("dp")
    for k, ref in zip(far_first(owners), out_refs):
        ref[...] = marked(selection((me ^ k) * capacity, capacity, place_ref[...]), x_ref[...])


def spread_dy_kernel(owners, capacity, place_ref, x_ref, dy_ref, *out_refs):
    me = lax.axis_index("dp")
    for k, ref in enumerate(out_refs):
        onehot = selection((me ^ k) * capacity, capacity, place_ref[...])
        if 0 < k < owners // 2:
            ref[:capacity] = marked(onehot, x_ref[...])
        ref[-capacity:] = selected(onehot, dy_ref[...])


def lookup_kernel(place_ref, out_ref):
    count = place_ref.shape[1]
    column = jnp.broadcast_to(place_ref[...].astype(F32), (LANES, count)).T[:, 0:1].astype(jnp.int32)
    out_ref[...] = (iota(out_ref.shape, 1) == column).astype(F32).astype(BF16)


def key_range(i):
    return max(0, (i * QUERIES - LONGEST + 1) // QUERIES) * QUERIES, (i + 1) * QUERIES


def by_head(rows, lane, half):
    heads = range(LANES // half)
    return jnp.concatenate(
        [jnp.where(lane // half == h, rows, jnp.zeros_like(rows)) for h in heads], axis=0
    )


def own_head(rows, lane, half):
    total = rows[:QUERIES]
    for h in range(1, LANES // half):
        total = jnp.where(lane // half == h, rows[h * QUERIES : (h + 1) * QUERIES], total)
    return total


def forward_kernel(owners, capacity, *refs):
    blocks = refs[:owners]
    users_ref, w_ref = refs[owners : owners + 2]
    (
        place_ref, unplace_ref, act_ref, slope_ref, xhat_ref, xhat_t_ref, x_rstd_ref,
        weights_ref, tangent_ref, nhat_ref, a_rstd_ref, gated_t_ref, q_t_ref, att_ref,
    ) = refs[owners + 2 :]
    me = lax.axis_index("dp")
    count, width = xhat_ref.shape
    half = width // HEADS
    valid = [blocks[k][:capacity, 0:LANES].astype(F32) != EMPTY for k in range(owners)]
    counts = [jnp.sum(v.astype(F32), axis=0, keepdims=True) for v in valid]
    source = iota((owners, LANES), 0) ^ me
    starts = jnp.zeros((owners, LANES), F32)
    for k in range(owners):
        starts = starts + jnp.where(source > (me ^ k), counts[k], 0.0)
    within = iota((capacity, LANES), 0).astype(F32)
    target = jnp.concatenate(
        [jnp.where(valid[k], starts[k : k + 1] + within, -1.0) for k in range(owners)], axis=0
    )
    target_t = target.T[0:1, :]
    slots = owners * capacity
    place = (iota((count, slots), 0) == target_t.astype(jnp.int32)).astype(F32).astype(BF16)
    place_ref[...] = place
    column = target[:, 0:1].astype(jnp.int32)
    unplace_ref[...] = (iota((slots, count), 1) == column).astype(F32).astype(BF16)
    received = jnp.concatenate([blocks[k][:capacity] for k in range(owners)], axis=0)
    x = dot(place, received)
    center = x - jnp.mean(x, axis=1, keepdims=True)
    rstd = lax.rsqrt(jnp.mean(center * center, axis=1, keepdims=True) + EPSILON)
    xhat32 = center * rstd
    xhat = xhat32.astype(BF16)
    xhat_ref[...] = xhat
    xhat_t_ref[...] = xhat32.T.astype(BF16)
    x_rstd_ref[...] = jnp.broadcast_to(rstd, (count, LANES))
    for part in range(4):
        columns = slice(part * width, (part + 1) * width)
        pre = dot(xhat, w_ref[:, columns])
        sig = 0.5 * jnp.tanh(0.5 * pre) + 0.5
        act = pre * sig
        act_ref[:, columns] = act.astype(BF16)
        slope_ref[:, columns] = (sig + act * (1.0 - sig)).astype(BF16)
        if part == 2:
            q_t_ref[...] = act.T.astype(BF16)
    users = users_ref[...]
    users_column = jnp.broadcast_to(users.astype(F32), (LANES, count)).T[:, 0:1].astype(jnp.int32)
    scale = half ** (-0.5)
    lane = iota((QUERIES, LANES), 1)
    for i in range(count // QUERIES):
        low, high = key_range(i)
        rows = slice(i * QUERIES, high)
        keep = (users_column[rows] == users[:, low:high]) & (
            iota((QUERIES, high - low), 1) + low <= iota((QUERIES, high - low), 0) + i * QUERIES
        )
        for pair in range(width // LANES):
            lanes = slice(pair * LANES, (pair + 1) * LANES)
            v = act_ref[low:high, width + lanes.start : width + lanes.stop]
            q = act_ref[rows, 2 * width + lanes.start : 2 * width + lanes.stop]
            k = act_ref[low:high, 3 * width + lanes.start : 3 * width + lanes.stop]
            scores = dot_nt(by_head(q, lane, half), k)
            weights = []
            for inner in range(LANES // half):
                head = pair * (LANES // half) + inner
                for r in range(0, QUERIES, BLOCK):
                    for c in range(low, high, BLOCK):
                        at = (slice(r, r + BLOCK), slice(c - low, c - low + BLOCK))
                        first = i * QUERIES + r
                        if c > first or c + LONGEST < first:
                            weights_ref[(head, i) + at] = jnp.zeros((BLOCK, BLOCK), BF16)
                            tangent_ref[(head, i) + at] = jnp.zeros((BLOCK, BLOCK), BF16)
                            continue
                        score = scores[inner * QUERIES + r : inner * QUERIES + r + BLOCK, at[1]]
                        sig = 0.5 * jnp.tanh(score * (0.5 * scale)) + 0.5
                        value = score * scale * sig
                        slope = (sig + value * (1.0 - sig)) * scale
                        weights_ref[(head, i) + at] = jnp.where(keep[at], value, 0.0).astype(BF16)
                        tangent_ref[(head, i) + at] = jnp.where(keep[at], slope, 0.0).astype(BF16)
                weights.append(weights_ref[head, i, :, 0 : high - low])
            att_ref[rows, lanes] = own_head(dot(jnp.concatenate(weights, axis=0), v), lane, half)
    attended = att_ref[...]
    center = attended - jnp.mean(attended, axis=1, keepdims=True)
    rstd = lax.rsqrt(jnp.mean(center * center, axis=1, keepdims=True) + EPSILON)
    nhat = center * rstd
    nhat_ref[...] = nhat.astype(BF16)
    a_rstd_ref[...] = jnp.broadcast_to(rstd, (count, LANES))
    gated_t_ref[...] = (nhat * act_ref[:, 0:width].astype(F32)).T.astype(BF16)


def fold(piece):
    rows, columns = piece.shape
    if columns >= LANES:
        return jnp.concatenate(
            [piece[:, c : c + LANES] for c in range(0, columns, LANES)], axis=0
        )
    step = rows * columns // LANES
    return jnp.concatenate([piece[r : r + step] for r in range(0, rows, step)], axis=1)


def unfold(piece, rows, columns):
    if columns >= LANES:
        return jnp.concatenate(
            [piece[r : r + rows] for r in range(0, piece.shape[0], rows)], axis=1
        )
    return jnp.concatenate(
        [piece[:, c : c + columns] for c in range(0, LANES, columns)], axis=0
    )


def attend_backward(
    pairs, act_ref, slope_ref, weights_ref, tangent_ref, q_t_ref, datt_ref, datt_t_ref,
    dpre_ref, dkv_t_ref,
):
    count, width = datt_ref.shape
    half = width // HEADS
    lane = iota((QUERIES, LANES), 1)
    steps = count // QUERIES
    heads = LANES // half
    for pair in pairs:
        lanes = slice(pair * LANES, (pair + 1) * LANES)
        dq = []
        dk_t = [[None] * steps for _ in range(heads)]
        dv_t = [[None] * steps for _ in range(heads)]
        for i in range(steps):
            low, high = key_range(i)
            rows = slice(i * QUERIES, high)
            v = act_ref[low:high, width + lanes.start : width + lanes.stop]
            k = act_ref[low:high, 3 * width + lanes.start : 3 * width + lanes.stop]
            dweight = dot_nt(by_head(datt_ref[rows, lanes], lane, half), v)
            dscore = []
            for inner in range(heads):
                head = pair * heads + inner
                own = slice(head * half, (head + 1) * half)
                tangent = tangent_ref[head, i, :, 0 : high - low].astype(F32)
                one = (dweight[inner * QUERIES : (inner + 1) * QUERIES] * tangent).astype(BF16)
                dscore.append(one)
                add_k = dot(q_t_ref[own, rows], one)
                add_v = dot(datt_t_ref[own, rows], weights_ref[head, i, :, 0 : high - low])
                for j in range(low // QUERIES, i + 1):
                    at = slice(j * QUERIES - low, (j + 1) * QUERIES - low)
                    for sums, add in ((dk_t[inner], add_k), (dv_t[inner], add_v)):
                        sums[j] = add[:, at] if sums[j] is None else sums[j] + add[:, at]
            dq.append(own_head(dot(jnp.concatenate(dscore, axis=0), k), lane, half))
        for inner in range(heads):
            for j in range(steps):
                at = slice(j * QUERIES, (j + 1) * QUERIES)
                dkv_t_ref[0, inner * half : (inner + 1) * half, at] = dv_t[inner][j]
                dkv_t_ref[1, inner * half : (inner + 1) * half, at] = dk_t[inner][j]
        for part, grad in (
            (1, dkv_t_ref[0].T),
            (2, jnp.concatenate(dq, axis=0)),
            (3, dkv_t_ref[1].T),
        ):
            columns = slice(part * width + lanes.start, part * width + lanes.stop)
            slope = slope_ref[:, columns].astype(F32)
            dpre_ref[:, columns] = (grad * slope).astype(BF16)


def cotangent_kernel(owners, capacity, *refs):
    blocks = refs[:owners]
    (
        place_ref, nhat_ref, a_rstd_ref, w_out_ref, act_ref, slope_ref,
        dy_ref, dpre_ref, datt_ref, datt_t_ref,
    ) = refs[owners:]
    width = dy_ref.shape[1]
    received = jnp.concatenate([blocks[k][-capacity:] for k in range(owners)], axis=0)
    dy = dot(place_ref[...], received).astype(BF16)
    dy_ref[...] = dy
    dgated = dot_nt(dy, w_out_ref[...])
    nhat = nhat_ref[...].astype(F32)
    dpre_ref[...] = (dgated * nhat * slope_ref[:, 0:width].astype(F32)).astype(BF16)
    dnhat = dgated * act_ref[:, 0:width].astype(F32)
    datt = a_rstd_ref[:, 0:1] * (
        dnhat
        - jnp.mean(dnhat, axis=1, keepdims=True)
        - nhat * jnp.mean(dnhat * nhat, axis=1, keepdims=True)
    )
    datt_ref[...] = datt.astype(BF16)
    datt_t_ref[...] = datt.T.astype(BF16)


def attention_kernel(dpre_u_ref, *refs):
    dpre_ref = refs[7]
    width = dpre_u_ref.shape[1]
    dpre_ref[:, 0:width] = dpre_u_ref[...]
    attend_backward(range(width // LANES), *refs)


def input_kernel(dpre_ref, w_ref, xhat_ref, x_rstd_ref, dy_ref, dx_ref):
    dxhat = dot_nt(dpre_ref[...], w_ref[...])
    xhat = xhat_ref[...].astype(F32)
    dx = dy_ref[...].astype(F32) + x_rstd_ref[:, 0:1] * (
        dxhat
        - jnp.mean(dxhat, axis=1, keepdims=True)
        - xhat * jnp.mean(dxhat * xhat, axis=1, keepdims=True)
    )
    dx_ref[...] = dx.astype(BF16)


def return_kernel(owners, capacity, dx_ref, unplace_ref, out_ref):
    me = lax.axis_index("dp")
    rows = dot(unplace_ref[...], dx_ref[...]).astype(BF16)
    for k in range(owners):
        at = pl.ds(pl.multiple_of((me ^ k) * capacity, capacity), capacity)
        out_ref[at, :] = rows[k * capacity : (k + 1) * capacity]


def term_rows(owners, groups, width):
    in_rows = width // groups * (4 * width // owners) // LANES
    return in_rows, width // groups * (width // owners) // LANES


def store_terms(grads, kept_ref, sent_ref, groups):
    group = lax.axis_index("rep")
    for r in range(groups):
        relative = group ^ r
        for target, ref in ((0, kept_ref), (1, sent_ref)):

            @pl.when((relative & 1) == target)
            def _():
                at = 0
                for grad in grads:
                    part = grad.shape[0] // groups
                    piece = fold(grad[r * part : (r + 1) * part]).astype(BF16)
                    ref[relative >> 1, at : at + piece.shape[0], :] = piece
                    at += piece.shape[0]


def columns_of(grad, owners_in):
    step = grad.shape[1] // owners_in
    return [grad[:, c : c + step] for c in range(0, grad.shape[1], step)]


def early_weight_kernel(
    owners, groups, xhat_t_ref, dpre_ref, gated_t_ref, dy_ref, kept_ref, sent_ref
):
    grads = columns_of(dot(xhat_t_ref[...], dpre_ref[...]), owners // 4)
    grads += columns_of(dot(gated_t_ref[...], dy_ref[...]), owners)
    store_terms(grads, kept_ref, sent_ref, groups)


def late_weight_kernel(owners, groups, xhat_t_ref, dpre_ref, kept_ref, sent_ref):
    width = xhat_t_ref.shape[0]
    grads = columns_of(dot(xhat_t_ref[...], dpre_ref[:, width:]), owners - owners // 4)
    store_terms(grads, kept_ref, sent_ref, groups)


def added(first, second):
    return first.astype(F32) + second.astype(F32)


def core_sum_kernel(kept_ref, got_ref, out_kept_ref, out_sent_ref):
    out_sent_ref[...] = added(kept_ref[1], got_ref[1]).astype(BF16)
    out_kept_ref[...] = added(kept_ref[0], got_ref[0]).astype(BF16)


def side_sum_kernel(owners, step, kept_ref, got_ref, out_kept_ref, out_sent_ref):
    me = lax.axis_index("dp")
    first = owners - kept_ref.shape[1] // step
    for d in range(first, owners):
        rows = slice((d - first) * step, (d - first + 1) * step)
        at = (d - first) // 2 * step
        term = added(kept_ref[:, rows, :], got_ref[:, rows, :]).astype(BF16)
        for target, ref in ((0, out_kept_ref), (1, out_sent_ref)):

            @pl.when(((me ^ d) & 1) == target)
            def _():
                ref[:, at : at + step, :] = term


def split_pairs(owners, sizes, first_ref, second_ref, kept_ref, sent_ref):
    me = lax.axis_index("dp")
    at = 0
    for number, step in sizes:
        base = at // 2
        for d in range(number):
            rows = slice(at, at + step)
            term = added(first_ref[rows, :], second_ref[rows, :]).astype(BF16)
            for target, ref in ((0, kept_ref), (1, sent_ref)):

                @pl.when(((me ^ d) & 1) == target)
                def _():
                    ref[base + d // 2 * step : base + (d // 2 + 1) * step, :] = term

            at += step


def plane_sum_kernel(owners, in_rows, out_rows, *refs):
    early_ref, early_got_ref, late_ref, late_got_ref = refs[:4]
    outs, total_ref = refs[4:-1], refs[-1]
    early = early_ref.shape[0]
    total_ref[:early] = added(early_ref[...], early_got_ref[...]).astype(BF16)
    total_ref[early:] = added(late_ref[...], late_got_ref[...]).astype(BF16)
    here = lax.axis_index("dp") >> 1
    quarter = owners // 8 * in_rows
    for k, ref in enumerate(outs):
        pair = here ^ k
        first = pair * in_rows
        first = jnp.where(first < quarter, first, first - quarter + early)
        ref[0:in_rows, :] = total_ref[pl.ds(pl.multiple_of(first, in_rows), in_rows), :]
        first = quarter + pair * out_rows
        ref[in_rows:, :] = total_ref[pl.ds(pl.multiple_of(first, out_rows), out_rows), :]


def total_kernel(*refs):
    total = refs[0][...].astype(F32)
    for ref in refs[1:-1]:
        total = total + ref[...].astype(F32)
    refs[-1][...] = total.astype(BF16)


def result_kernel(groups, in_rows, *refs):
    in_ref, out_ref = refs[groups:]
    group = lax.axis_index("rep")
    part = in_ref.shape[0] // groups
    for k in range(groups):
        rows = pl.ds(pl.multiple_of((group ^ k) * part, part), part)
        piece = refs[k][...].astype(F32)
        in_ref[rows, :] = unfold(piece[:in_rows], part, in_ref.shape[1])
        out_ref[:, rows] = unfold(piece[in_rows:], part, out_ref.shape[0]).T


def collect_kernel(lookup_ref, rows_ref, out_ref):
    out_ref[...] = dot(lookup_ref[...], rows_ref[...]).astype(BF16)


def swap(value, axis, distance):
    size = lax.axis_size(axis)
    return lax.ppermute(value, axis, [(i, i ^ distance) for i in range(size)])


def ordered(value, *earlier):
    return lax.optimization_barrier((value,) + earlier)[0]


def exchange(far_x, blocks):
    owners = len(blocks)
    got_x, got = list(blocks), list(blocks)
    for k, block in zip(far_first(owners), far_x):
        got_x[k] = swap(block, "dp", k) if k else block
    for k in range(1, owners):
        if k < owners // 2:
            got_x[k] = got[k] = swap(blocks[k], "dp", k)
        else:
            got[k] = swap(ordered(blocks[k], got_x[k ^ 1]), "dp", k)
    return got_x, got


def on_device(events, grad_out, w_uvqk, w_out, send_place, send_counts, user_ids):
    owners = lax.axis_size("dp")
    groups = lax.axis_size("rep")
    count, width = events.shape
    capacity = 2 * count // owners
    slots = owners * capacity
    steps = count // QUERIES
    spans = max(high - low for low, high in map(key_range, range(steps)))
    route = 2 * slots * count * width
    square = shape((count, width))
    square_t = shape((width, count))
    wide = shape((count, 4 * width))
    column = shape((count, LANES), F32)
    scores = shape((HEADS, steps, QUERIES, spans))
    project = 2 * count * width * 4 * width
    attend = 2 * count * spans * width

    far_x = call(
        functools.partial(spread_x_kernel, owners, capacity),
        [shape((capacity, width))] * (owners // 2 + 1), send_place, events, flops=route // 2,
    )
    blocks = call(
        functools.partial(spread_dy_kernel, owners, capacity),
        [
            shape(((2 if 0 < k < owners // 2 else 1) * capacity, width))
            for k in range(owners)
        ],
        send_place, events, grad_out, flops=route,
    )
    lookup = call(lookup_kernel, shape((count, slots)), send_place)
    x_blocks, dy_blocks = exchange(far_x, blocks)
    (
        place, unplace, act, slope, xhat, xhat_t, x_rstd,
        weights, tangent, nhat, a_rstd, gated_t, q_t,
    ) = call(
        functools.partial(forward_kernel, owners, capacity),
        [
            shape((count, slots)), shape((slots, count)), wide, wide, square, square_t, column,
            scores, scores, square, column, square_t, square_t,
        ],
        *x_blocks, user_ids, w_uvqk,
        flops=route + project + 2 * attend, transcendentals=HEADS * count * spans,
        scratch=[pltpu.VMEM((count, width), F32)], vmem=28,
    )
    owned_dy, dpre_u, datt, datt_t = call(
        functools.partial(cotangent_kernel, owners, capacity),
        [square, square, square, square_t],
        *dy_blocks, place, nhat, a_rstd, w_out, act, slope, flops=route + project // 4,
    )
    in_rows, out_rows = term_rows(owners, groups, width)
    early_sizes = ((owners // 4, in_rows), (owners, out_rows))
    late_sizes = ((owners - owners // 4, in_rows),)
    early, late = (sum(n * rows for n, rows in sizes) for sizes in (early_sizes, late_sizes))
    early_kept, early_sent = call(
        functools.partial(early_weight_kernel, owners, groups),
        [shape((2, early, LANES))] * 2, xhat_t, dpre_u, gated_t, owned_dy, flops=project // 2,
    )
    dpre = call(
        attention_kernel, wide,
        dpre_u, act, slope, weights, tangent, q_t, ordered(datt, early_sent), datt_t,
        flops=4 * attend, scratch=[pltpu.VMEM((2, LANES, count), F32)], vmem=28,
    )
    early_kept, early_sent = call(
        core_sum_kernel, [shape((early, LANES))] * 2, early_kept, swap(early_sent, "rep", 1)
    )
    early_got = swap(early_sent, "rep", 2)
    late_kept, late_sent = call(
        functools.partial(late_weight_kernel, owners, groups),
        [shape((2, late, LANES))] * 2, xhat_t, ordered(dpre, early_sent), flops=project,
    )
    dx = call(
        input_kernel, square, ordered(dpre, late_sent), w_uvqk, xhat, x_rstd, owned_dy,
        flops=project,
    )
    late_kept, late_sent = call(
        functools.partial(side_sum_kernel, owners, in_rows), [shape((2, late // 2, LANES))] * 2,
        late_kept, swap(late_sent, "rep", 1),
    )
    back = call(
        functools.partial(return_kernel, owners, capacity), shape((slots, width)),
        ordered(dx, late_sent), unplace, flops=route,
    )
    late_got = swap(late_sent, "dp", 1)
    back = lax.all_to_all(back, "dp", split_axis=0, concat_axis=0, tiled=True)
    early_kept, early_sent = call(
        functools.partial(split_pairs, owners, early_sizes), [shape((early // 2, LANES))] * 2,
        early_kept, early_got, flops=WAITING,
    )
    late_kept, late_sent = call(
        core_sum_kernel, [shape((late // 2, LANES))] * 2, late_kept, late_got, flops=WAITING,
    )
    pairs = owners // 2
    rows = in_rows + out_rows
    pieces = call(
        functools.partial(plane_sum_kernel, owners, in_rows, out_rows),
        [shape((rows, LANES))] * pairs,
        early_kept, swap(early_sent, "dp", 1), late_kept, swap(late_sent, "rep", 2),
        flops=WAITING, scratch=[pltpu.VMEM(((early + late) // 2, LANES), BF16)],
    )
    pieces = [pieces[0]] + [swap(pieces[k], "dp", 2 * k) for k in range(1, pairs)]
    own = call(total_kernel, shape((rows, LANES)), *pieces, flops=WAITING)
    far = swap(own, "rep", 2)
    shares = [own, swap(own, "rep", 1), far, swap(far, "rep", 1)]
    grad_events = call(collect_kernel, square, lookup, back, flops=route)
    shares[0] = ordered(own, grad_events)
    share_in, share_out = call(
        functools.partial(result_kernel, groups, in_rows),
        [shape((width, 4 * width // owners), F32), shape((width // owners, width), F32)],
        *shares, flops=WAITING,
    )
    return (grad_events, share_in, share_out.T)


def solution(mesh):
    return jax.shard_map(
        on_device,
        mesh=mesh,
        in_specs=(
            P(("dp", "rep"), None),
            P(("dp", "rep"), None),
            P(),
            P(),
            P(("dp", "rep"), None),
            P(("dp", "rep"), None),
            P(("dp", "rep"), None),
        ),
        out_specs=(P(("dp", "rep"), None), P(None, "dp"), P(None, "dp")),
        check_vma=False,
    )
```

```python
import functools

import jax
import jax.numpy as jnp
from jax import lax
from jax.experimental import pallas as pl
from jax.experimental.pallas import tpu as pltpu
from jax.sharding import PartitionSpec as P

HEADS = 8
LONGEST = 256
EPSILON = 1e-05
EMPTY = 128.0
BLOCK = 128
QUERIES = 256
LANES = 128
F32 = jnp.float32
WAITING = 3 * 10**9
BF16 = jnp.bfloat16


def dot(a, b):
    return jnp.dot(a, b, preferred_element_type=F32)


def dot_nt(a, b):
    return lax.dot_general(a, b, (((1,), (1,)), ((), ())), preferred_element_type=F32)


def iota(shape, dim):
    return lax.broadcasted_iota(jnp.int32, shape, dim)


def call(kernel, out_shape, *args, flops=0, transcendentals=0, scratch=(), vmem=16):
    moved = sum(a.size * a.dtype.itemsize for a in args)
    moved += sum(o.size * o.dtype.itemsize for o in jax.tree.leaves(out_shape))
    return pl.pallas_call(
        kernel,
        out_shape=out_shape,
        scratch_shapes=scratch,
        compiler_params=pltpu.CompilerParams(vmem_limit_bytes=vmem * 1024 * 1024),
        cost_estimate=pl.CostEstimate(
            flops=flops, bytes_accessed=moved, transcendentals=transcendentals
        ),
    )(*args)


def shape(dims, dtype=BF16):
    return jax.ShapeDtypeStruct(tuple(dims), dtype)


def far_first(owners):
    return [0, *range(owners // 2, owners)]


def selection(first, capacity, place):
    return (iota((capacity, place.shape[1]), 0) + first == place).astype(F32)


def selected(onehot, rows):
    return dot(onehot.astype(BF16), rows).astype(BF16)


def marked(onehot, rows):
    block = dot(onehot.astype(BF16), rows)
    return (block + (1.0 - jnp.sum(onehot, axis=1, keepdims=True)) * EMPTY).astype(BF16)


def spread_x_kernel(owners, capacity, place_ref, x_ref, *out_refs):
    me = lax.axis_index("dp")
    for k, ref in zip(far_first(owners), out_refs):
        ref[...] = marked(selection((me ^ k) * capacity, capacity, place_ref[...]), x_ref[...])


def spread_dy_kernel(owners, capacity, place_ref, x_ref, dy_ref, *out_refs):
    me = lax.axis_index("dp")
    for k, ref in enumerate(out_refs):
        onehot = selection((me ^ k) * capacity, capacity, place_ref[...])
        if 0 < k < owners // 2:
            ref[:capacity] = marked(onehot, x_ref[...])
        ref[-capacity:] = selected(onehot, dy_ref[...])


def lookup_kernel(place_ref, out_ref):
    count = place_ref.shape[1]
    column = jnp.broadcast_to(place_ref[...].astype(F32), (LANES, count)).T[:, 0:1].astype(jnp.int32)
    out_ref[...] = (iota(out_ref.shape, 1) == column).astype(F32).astype(BF16)


def key_range(i):
    return max(0, (i * QUERIES - LONGEST + 1) // QUERIES) * QUERIES, (i + 1) * QUERIES


def by_head(rows, lane, half):
    heads = range(LANES // half)
    return jnp.concatenate(
        [jnp.where(lane // half == h, rows, jnp.zeros_like(rows)) for h in heads], axis=0
    )


def own_head(rows, lane, half):
    total = rows[:QUERIES]
    for h in range(1, LANES // half):
        total = jnp.where(lane // half == h, rows[h * QUERIES : (h + 1) * QUERIES], total)
    return total


def forward_kernel(owners, capacity, *refs):
    blocks = refs[:owners]
    users_ref, w_ref = refs[owners : owners + 2]
    (
        place_ref, unplace_ref, act_ref, slope_ref, xhat_ref, xhat_t_ref, x_rstd_ref,
        weights_ref, tangent_ref, nhat_ref, a_rstd_ref, gated_t_ref, q_t_ref, att_ref,
    ) = refs[owners + 2 :]
    me = lax.axis_index("dp")
    count, width = xhat_ref.shape
    half = width // HEADS
    valid = [blocks[k][:capacity, 0:LANES].astype(F32) != EMPTY for k in range(owners)]
    counts = [jnp.sum(v.astype(F32), axis=0, keepdims=True) for v in valid]
    source = iota((owners, LANES), 0) ^ me
    starts = jnp.zeros((owners, LANES), F32)
    for k in range(owners):
        starts = starts + jnp.where(source > (me ^ k), counts[k], 0.0)
    within = iota((capacity, LANES), 0).astype(F32)
    target = jnp.concatenate(
        [jnp.where(valid[k], starts[k : k + 1] + within, -1.0) for k in range(owners)], axis=0
    )
    target_t = target.T[0:1, :]
    slots = owners * capacity
    place = (iota((count, slots), 0) == target_t.astype(jnp.int32)).astype(F32).astype(BF16)
    place_ref[...] = place
    column = target[:, 0:1].astype(jnp.int32)
    unplace_ref[...] = (iota((slots, count), 1) == column).astype(F32).astype(BF16)
    received = jnp.concatenate([blocks[k][:capacity] for k in range(owners)], axis=0)
    x = dot(place, received)
    center = x - jnp.mean(x, axis=1, keepdims=True)
    rstd = lax.rsqrt(jnp.mean(center * center, axis=1, keepdims=True) + EPSILON)
    xhat32 = center * rstd
    xhat = xhat32.astype(BF16)
    xhat_ref[...] = xhat
    xhat_t_ref[...] = xhat32.T.astype(BF16)
    x_rstd_ref[...] = jnp.broadcast_to(rstd, (count, LANES))
    for part in range(4):
        columns = slice(part * width, (part + 1) * width)
        pre = dot(xhat, w_ref[:, columns])
        sig = 0.5 * jnp.tanh(0.5 * pre) + 0.5
        act = pre * sig
        act_ref[:, columns] = act.astype(BF16)
        slope_ref[:, columns] = (sig + act * (1.0 - sig)).astype(BF16)
        if part == 2:
            q_t_ref[...] = act.T.astype(BF16)
    users = users_ref[...]
    users_column = jnp.broadcast_to(users.astype(F32), (LANES, count)).T[:, 0:1].astype(jnp.int32)
    scale = half ** (-0.5)
    lane = iota((QUERIES, LANES), 1)
    for i in range(count // QUERIES):
        low, high = key_range(i)
        rows = slice(i * QUERIES, high)
        keep = (users_column[rows] == users[:, low:high]) & (
            iota((QUERIES, high - low), 1) + low <= iota((QUERIES, high - low), 0) + i * QUERIES
        )
        for pair in range(width // LANES):
            lanes = slice(pair * LANES, (pair + 1) * LANES)
            v = act_ref[low:high, width + lanes.start : width + lanes.stop]
            q = act_ref[rows, 2 * width + lanes.start : 2 * width + lanes.stop]
            k = act_ref[low:high, 3 * width + lanes.start : 3 * width + lanes.stop]
            scores = dot_nt(by_head(q, lane, half), k)
            weights = []
            for inner in range(LANES // half):
                head = pair * (LANES // half) + inner
                for r in range(0, QUERIES, BLOCK):
                    for c in range(low, high, BLOCK):
                        at = (slice(r, r + BLOCK), slice(c - low, c - low + BLOCK))
                        first = i * QUERIES + r
                        if c > first or c + LONGEST < first:
                            weights_ref[(head, i) + at] = jnp.zeros((BLOCK, BLOCK), BF16)
                            tangent_ref[(head, i) + at] = jnp.zeros((BLOCK, BLOCK), BF16)
                            continue
                        score = scores[inner * QUERIES + r : inner * QUERIES + r + BLOCK, at[1]]
                        sig = 0.5 * jnp.tanh(score * (0.5 * scale)) + 0.5
                        value = score * scale * sig
                        slope = (sig + value * (1.0 - sig)) * scale
                        weights_ref[(head, i) + at] = jnp.where(keep[at], value, 0.0).astype(BF16)
                        tangent_ref[(head, i) + at] = jnp.where(keep[at], slope, 0.0).astype(BF16)
                weights.append(weights_ref[head, i, :, 0 : high - low])
            att_ref[rows, lanes] = own_head(dot(jnp.concatenate(weights, axis=0), v), lane, half)
    attended = att_ref[...]
    center = attended - jnp.mean(attended, axis=1, keepdims=True)
    rstd = lax.rsqrt(jnp.mean(center * center, axis=1, keepdims=True) + EPSILON)
    nhat = center * rstd
    nhat_ref[...] = nhat.astype(BF16)
    a_rstd_ref[...] = jnp.broadcast_to(rstd, (count, LANES))
    gated_t_ref[...] = (nhat * act_ref[:, 0:width].astype(F32)).T.astype(BF16)


def fold(piece):
    rows, columns = piece.shape
    if columns >= LANES:
        return jnp.concatenate(
            [piece[:, c : c + LANES] for c in range(0, columns, LANES)], axis=0
        )
    step = rows * columns // LANES
    return jnp.concatenate([piece[r : r + step] for r in range(0, rows, step)], axis=1)


def unfold(piece, rows, columns):
    if columns >= LANES:
        return jnp.concatenate(
            [piece[r : r + rows] for r in range(0, piece.shape[0], rows)], axis=1
        )
    return jnp.concatenate(
        [piece[:, c : c + columns] for c in range(0, LANES, columns)], axis=0
    )


def attend_backward(
    pairs, act_ref, slope_ref, weights_ref, tangent_ref, q_t_ref, datt_ref, datt_t_ref,
    dpre_ref, dkv_t_ref,
):
    count, width = datt_ref.shape
    half = width // HEADS
    lane = iota((QUERIES, LANES), 1)
    steps = count // QUERIES
    heads = LANES // half
    for pair in pairs:
        lanes = slice(pair * LANES, (pair + 1) * LANES)
        dq = []
        dk_t = [[None] * steps for _ in range(heads)]
        dv_t = [[None] * steps for _ in range(heads)]
        for i in range(steps):
            low, high = key_range(i)
            rows = slice(i * QUERIES, high)
            v = act_ref[low:high, width + lanes.start : width + lanes.stop]
            k = act_ref[low:high, 3 * width + lanes.start : 3 * width + lanes.stop]
            dweight = dot_nt(by_head(datt_ref[rows, lanes], lane, half), v)
            dscore = []
            for inner in range(heads):
                head = pair * heads + inner
                own = slice(head * half, (head + 1) * half)
                tangent = tangent_ref[head, i, :, 0 : high - low].astype(F32)
                one = (dweight[inner * QUERIES : (inner + 1) * QUERIES] * tangent).astype(BF16)
                dscore.append(one)
                add_k = dot(q_t_ref[own, rows], one)
                add_v = dot(datt_t_ref[own, rows], weights_ref[head, i, :, 0 : high - low])
                for j in range(low // QUERIES, i + 1):
                    at = slice(j * QUERIES - low, (j + 1) * QUERIES - low)
                    for sums, add in ((dk_t[inner], add_k), (dv_t[inner], add_v)):
                        sums[j] = add[:, at] if sums[j] is None else sums[j] + add[:, at]
            dq.append(own_head(dot(jnp.concatenate(dscore, axis=0), k), lane, half))
        for inner in range(heads):
            for j in range(steps):
                at = slice(j * QUERIES, (j + 1) * QUERIES)
                dkv_t_ref[0, inner * half : (inner + 1) * half, at] = dv_t[inner][j].astype(BF16)
                dkv_t_ref[1, inner * half : (inner + 1) * half, at] = dk_t[inner][j].astype(BF16)
        for part, grad in (
            (1, dkv_t_ref[0].T),
            (2, jnp.concatenate(dq, axis=0)),
            (3, dkv_t_ref[1].T),
        ):
            columns = slice(part * width + lanes.start, part * width + lanes.stop)
            slope = slope_ref[:, columns].astype(F32)
            dpre_ref[:, columns] = (grad.astype(F32) * slope).astype(BF16)


def cotangent_kernel(owners, capacity, *refs):
    blocks = refs[:owners]
    (
        place_ref, nhat_ref, a_rstd_ref, w_out_ref, act_ref, slope_ref,
        dy_ref, dpre_ref, datt_ref, datt_t_ref,
    ) = refs[owners:]
    width = dy_ref.shape[1]
    received = jnp.concatenate([blocks[k][-capacity:] for k in range(owners)], axis=0)
    dy = dot(place_ref[...], received).astype(BF16)
    dy_ref[...] = dy
    dgated = dot_nt(dy, w_out_ref[...])
    nhat = nhat_ref[...].astype(F32)
    dpre_ref[...] = (dgated * nhat * slope_ref[:, 0:width].astype(F32)).astype(BF16)
    dnhat = dgated * act_ref[:, 0:width].astype(F32)
    datt = a_rstd_ref[:, 0:1] * (
        dnhat
        - jnp.mean(dnhat, axis=1, keepdims=True)
        - nhat * jnp.mean(dnhat * nhat, axis=1, keepdims=True)
    )
    datt_ref[...] = datt.astype(BF16)
    datt_t_ref[...] = datt.astype(BF16).T


def attention_kernel(dpre_u_ref, *refs):
    dpre_ref = refs[7]
    width = dpre_u_ref.shape[1]
    dpre_ref[:, 0:width] = dpre_u_ref[...]
    attend_backward(range(width // LANES), *refs)


def input_kernel(dpre_ref, w_ref, xhat_ref, x_rstd_ref, dy_ref, dx_ref):
    dxhat = dot_nt(dpre_ref[...], w_ref[...])
    xhat = xhat_ref[...].astype(F32)
    dx = dy_ref[...].astype(F32) + x_rstd_ref[:, 0:1] * (
        dxhat
        - jnp.mean(dxhat, axis=1, keepdims=True)
        - xhat * jnp.mean(dxhat * xhat, axis=1, keepdims=True)
    )
    dx_ref[...] = dx.astype(BF16)


def return_kernel(owners, capacity, dx_ref, unplace_ref, out_ref):
    me = lax.axis_index("dp")
    rows = dot(unplace_ref[...], dx_ref[...]).astype(BF16)
    for k in range(owners):
        at = pl.ds(pl.multiple_of((me ^ k) * capacity, capacity), capacity)
        out_ref[at, :] = rows[k * capacity : (k + 1) * capacity]


def term_rows(owners, groups, width):
    in_rows = width // groups * (4 * width // owners) // LANES
    return in_rows, width // groups * (width // owners) // LANES


def store_terms(grads, kept_ref, sent_ref, groups):
    group = lax.axis_index("rep")
    for r in range(groups):
        relative = group ^ r
        for target, ref in ((0, kept_ref), (1, sent_ref)):

            @pl.when((relative & 1) == target)
            def _():
                at = 0
                for grad in grads:
                    part = grad.shape[0] // groups
                    piece = fold(grad[r * part : (r + 1) * part]).astype(BF16)
                    ref[relative >> 1, at : at + piece.shape[0], :] = piece
                    at += piece.shape[0]


def columns_of(grad, owners_in):
    step = grad.shape[1] // owners_in
    return [grad[:, c : c + step] for c in range(0, grad.shape[1], step)]


def early_weight_kernel(
    owners, groups, xhat_t_ref, dpre_ref, gated_t_ref, dy_ref, kept_ref, sent_ref
):
    grads = columns_of(dot(xhat_t_ref[...], dpre_ref[...]), owners // 4)
    grads += columns_of(dot(gated_t_ref[...], dy_ref[...]), owners)
    store_terms(grads, kept_ref, sent_ref, groups)


def late_weight_kernel(owners, groups, xhat_t_ref, dpre_ref, kept_ref, sent_ref):
    width = xhat_t_ref.shape[0]
    grads = columns_of(dot(xhat_t_ref[...], dpre_ref[:, width:]), owners - owners // 4)
    store_terms(grads, kept_ref, sent_ref, groups)


def added(first, second):
    return first.astype(F32) + second.astype(F32)


def core_sum_kernel(kept_ref, got_ref, out_kept_ref, out_sent_ref):
    out_sent_ref[...] = added(kept_ref[1], got_ref[1]).astype(BF16)
    out_kept_ref[...] = added(kept_ref[0], got_ref[0]).astype(BF16)


def side_sum_kernel(owners, step, kept_ref, got_ref, out_kept_ref, out_sent_ref):
    me = lax.axis_index("dp")
    first = owners - kept_ref.shape[1] // step
    for d in range(first, owners):
        rows = slice((d - first) * step, (d - first + 1) * step)
        at = (d - first) // 2 * step
        term = added(kept_ref[:, rows, :], got_ref[:, rows, :]).astype(BF16)
        for target, ref in ((0, out_kept_ref), (1, out_sent_ref)):

            @pl.when(((me ^ d) & 1) == target)
            def _():
                ref[:, at : at + step, :] = term


def split_pairs(owners, sizes, first_ref, second_ref, kept_ref, sent_ref):
    me = lax.axis_index("dp")
    at = 0
    for number, step in sizes:
        base = at // 2
        for d in range(number):
            rows = slice(at, at + step)
            term = added(first_ref[rows, :], second_ref[rows, :]).astype(BF16)
            for target, ref in ((0, kept_ref), (1, sent_ref)):

                @pl.when(((me ^ d) & 1) == target)
                def _():
                    ref[base + d // 2 * step : base + (d // 2 + 1) * step, :] = term

            at += step


def plane_sum_kernel(owners, in_rows, out_rows, *refs):
    early_ref, early_got_ref, late_ref, late_got_ref = refs[:4]
    outs, total_ref = refs[4:-1], refs[-1]
    early = early_ref.shape[0]
    total_ref[:early] = added(early_ref[...], early_got_ref[...]).astype(BF16)
    total_ref[early:] = added(late_ref[...], late_got_ref[...]).astype(BF16)
    here = lax.axis_index("dp") >> 1
    quarter = owners // 8 * in_rows
    for k, ref in enumerate(outs):
        pair = here ^ k
        first = pair * in_rows
        first = jnp.where(first < quarter, first, first - quarter + early)
        ref[0:in_rows, :] = total_ref[pl.ds(pl.multiple_of(first, in_rows), in_rows), :]
        first = quarter + pair * out_rows
        ref[in_rows:, :] = total_ref[pl.ds(pl.multiple_of(first, out_rows), out_rows), :]


def total_kernel(*refs):
    total = refs[0][...].astype(F32)
    for ref in refs[1:-1]:
        total = total + ref[...].astype(F32)
    refs[-1][...] = total.astype(BF16)


def result_kernel(groups, in_rows, *refs):
    in_ref, out_ref = refs[groups:]
    group = lax.axis_index("rep")
    part = in_ref.shape[0] // groups
    for k in range(groups):
        rows = pl.ds(pl.multiple_of((group ^ k) * part, part), part)
        piece = refs[k][...].astype(F32)
        in_ref[rows, :] = unfold(piece[:in_rows], part, in_ref.shape[1])
        out_ref[:, rows] = unfold(piece[in_rows:], part, out_ref.shape[0]).T


def collect_kernel(lookup_ref, rows_ref, out_ref):
    out_ref[...] = dot(lookup_ref[...], rows_ref[...]).astype(BF16)


def swap(value, axis, distance):
    size = lax.axis_size(axis)
    return lax.ppermute(value, axis, [(i, i ^ distance) for i in range(size)])


def ordered(value, *earlier):
    return lax.optimization_barrier((value,) + earlier)[0]


def exchange(far_x, blocks):
    owners = len(blocks)
    got_x, got = list(blocks), list(blocks)
    for k, block in zip(far_first(owners), far_x):
        got_x[k] = swap(block, "dp", k) if k else block
    for k in range(1, owners):
        if k < owners // 2:
            got_x[k] = got[k] = swap(blocks[k], "dp", k)
        else:
            got[k] = swap(ordered(blocks[k], got_x[k ^ 1]), "dp", k)
    return got_x, got


def on_device(events, grad_out, w_uvqk, w_out, send_place, send_counts, user_ids):
    owners = lax.axis_size("dp")
    groups = lax.axis_size("rep")
    count, width = events.shape
    capacity = 2 * count // owners
    slots = owners * capacity
    steps = count // QUERIES
    spans = max(high - low for low, high in map(key_range, range(steps)))
    route = 2 * slots * count * width
    square = shape((count, width))
    square_t = shape((width, count))
    wide = shape((count, 4 * width))
    column = shape((count, LANES), F32)
    scores = shape((HEADS, steps, QUERIES, spans))
    project = 2 * count * width * 4 * width
    attend = 2 * count * spans * width

    far_x = call(
        functools.partial(spread_x_kernel, owners, capacity),
        [shape((capacity, width))] * (owners // 2 + 1), send_place, events, flops=route // 2,
    )
    blocks = call(
        functools.partial(spread_dy_kernel, owners, capacity),
        [
            shape(((2 if 0 < k < owners // 2 else 1) * capacity, width))
            for k in range(owners)
        ],
        send_place, events, grad_out, flops=route,
    )
    lookup = call(lookup_kernel, shape((count, slots)), send_place)
    x_blocks, dy_blocks = exchange(far_x, blocks)
    (
        place, unplace, act, slope, xhat, xhat_t, x_rstd,
        weights, tangent, nhat, a_rstd, gated_t, q_t,
    ) = call(
        functools.partial(forward_kernel, owners, capacity),
        [
            shape((count, slots)), shape((slots, count)), wide, wide, square, square_t, column,
            scores, scores, square, column, square_t, square_t,
        ],
        *x_blocks, user_ids, w_uvqk,
        flops=route + project + 2 * attend, transcendentals=HEADS * count * spans,
        scratch=[pltpu.VMEM((count, width), F32)], vmem=28,
    )
    owned_dy, dpre_u, datt, datt_t = call(
        functools.partial(cotangent_kernel, owners, capacity),
        [square, square, square, square_t],
        *dy_blocks, place, nhat, a_rstd, w_out, act, slope, flops=route + project // 4,
    )
    in_rows, out_rows = term_rows(owners, groups, width)
    early_sizes = ((owners // 4, in_rows), (owners, out_rows))
    late_sizes = ((owners - owners // 4, in_rows),)
    early, late = (sum(n * rows for n, rows in sizes) for sizes in (early_sizes, late_sizes))
    early_kept, early_sent = call(
        functools.partial(early_weight_kernel, owners, groups),
        [shape((2, early, LANES))] * 2, xhat_t, dpre_u, gated_t, owned_dy, flops=project // 2,
    )
    dpre = call(
        attention_kernel, wide,
        dpre_u, act, slope, weights, tangent, q_t, ordered(datt, early_sent), datt_t,
        flops=4 * attend, scratch=[pltpu.VMEM((2, LANES, count), BF16)], vmem=28,
    )
    early_kept, early_sent = call(
        core_sum_kernel, [shape((early, LANES))] * 2, early_kept, swap(early_sent, "rep", 1)
    )
    early_got = swap(early_sent, "rep", 2)
    late_kept, late_sent = call(
        functools.partial(late_weight_kernel, owners, groups),
        [shape((2, late, LANES))] * 2, xhat_t, ordered(dpre, early_sent), flops=project,
    )
    dx = call(
        input_kernel, square, ordered(dpre, late_sent), w_uvqk, xhat, x_rstd, owned_dy,
        flops=project,
    )
    late_kept, late_sent = call(
        functools.partial(side_sum_kernel, owners, in_rows), [shape((2, late // 2, LANES))] * 2,
        late_kept, swap(late_sent, "rep", 1),
    )
    back = call(
        functools.partial(return_kernel, owners, capacity), shape((slots, width)),
        ordered(dx, late_sent), unplace, flops=route,
    )
    late_got = swap(late_sent, "dp", 1)
    back = lax.all_to_all(back, "dp", split_axis=0, concat_axis=0, tiled=True)
    early_kept, early_sent = call(
        functools.partial(split_pairs, owners, early_sizes), [shape((early // 2, LANES))] * 2,
        early_kept, early_got, flops=WAITING,
    )
    late_kept, late_sent = call(
        core_sum_kernel, [shape((late // 2, LANES))] * 2, late_kept, late_got, flops=WAITING,
    )
    pairs = owners // 2
    rows = in_rows + out_rows
    pieces = call(
        functools.partial(plane_sum_kernel, owners, in_rows, out_rows),
        [shape((rows, LANES))] * pairs,
        early_kept, swap(early_sent, "dp", 1), late_kept, swap(late_sent, "rep", 2),
        flops=WAITING, scratch=[pltpu.VMEM(((early + late) // 2, LANES), BF16)],
    )
    pieces = [pieces[0]] + [swap(pieces[k], "dp", 2 * k) for k in range(1, pairs)]
    own = call(total_kernel, shape((rows, LANES)), *pieces, flops=WAITING)
    far = swap(own, "rep", 2)
    shares = [own, swap(own, "rep", 1), far, swap(far, "rep", 1)]
    grad_events = call(collect_kernel, square, lookup, back, flops=route)
    shares[0] = ordered(own, grad_events)
    share_in, share_out = call(
        functools.partial(result_kernel, groups, in_rows),
        [shape((width, 4 * width // owners), F32), shape((width // owners, width), F32)],
        *shares, flops=WAITING,
    )
    return (grad_events, share_in, share_out.T)


def solution(mesh):
    return jax.shard_map(
        on_device,
        mesh=mesh,
        in_specs=(
            P(("dp", "rep"), None),
            P(("dp", "rep"), None),
            P(),
            P(),
            P(("dp", "rep"), None),
            P(("dp", "rep"), None),
            P(("dp", "rep"), None),
        ),
        out_specs=(P(("dp", "rep"), None), P(None, "dp"), P(None, "dp")),
        check_vma=False,
    )
```
